512 devices in a mesh: band: 8 (over y, x_hi), pw: 64 (over z, x_lo, core).
Axes of the slice: x: 4 (x_hi: 2, x_lo: 2; x = x_hi * 2 + x_lo), y: 4, z: 16, core: 2. Of those that a mesh axis runs over, the one named last changes fastest.
Arguments:
- block: bfloat16 [64, 2, 2560, 128], P('band', None, 'pw'), may hold values from -6 to 6
- bands: bfloat16 [256, 2, 2560, 128], P('band', None, 'pw'), may hold values from -0.01953125 to 0.01953125
- potential: float32 [128, 128, 128], P('pw'), may hold values from -4 to 1
- stick_cells: int32 [2560], P('pw'), may hold values from 0 to 16383, as said below
- sphere_mask: int32 [2560, 128], P('pw'), may hold values from 0 to 1, as said below
Outputs:
- applied: bfloat16 [64, 2, 2560, 128], P('band', None, 'pw')
- correlation: float32 [2, 256, 64], P(None, 'band')
- subspace: float32 [2, 256, 64], P(None, 'band')
The draws below stay inside these ranges and needn't reach their ends.
Inputs may be any that keep to these rules, and one draw needn't show every extreme that they name: `stick_cells`: the 2560 distinct columns with the smallest g(x)^2 + g(y)^2, ties in random order, placed in random order over the sticks. `sphere_mask`: 1 exactly where g(cx)^2 + g(cy)^2 + g(k)^2 <= 32^2 for stick s's column (cx, cy) and index k, else 0.
All inputs are finite; a program needn't handle non-finite values.
Results may differ from the reference program's by a relative error of at most 0.002.
Values may be sent and summed in bfloat16 or wider, within the bound.
No kernel may reach another device: no remote copies, remote signals or barrier semaphores. Data moves between devices by JAX's collectives and lax.ppermute only.
A program may use at most 128 MiB of HBM per device.

```python
import jax
import jax.numpy as jnp
from jax import lax

NG = 128
NSTK = 2560
RAD = 32
BLOCK = 64
NB_ALL = 256
ZPAD = 128


def signed_frequency_drawn(index, period):
    return jnp.where(index < period // 2, index, index - period)


def nearest_sticks(key):
    flat = jnp.arange(NG * NG, dtype=jnp.int32)
    freq_x = signed_frequency_drawn(flat // NG, NG)
    freq_y = signed_frequency_drawn(flat % NG, NG)
    radial = freq_x * freq_x + freq_y * freq_y
    jitter = jax.random.randint(key, (NG * NG,), 0, 65536, dtype=jnp.int32)
    scores = radial * 65536 + jitter
    chosen = jnp.argsort(scores, stable=True)[:NSTK].astype(jnp.int32)
    shuffle = jax.random.permutation(jax.random.fold_in(key, 7), NSTK)
    return chosen[shuffle].astype(jnp.int32)


def draw_stick_cells(key, part):
    cells = nearest_sticks(key)
    return cells


def draw_sphere_mask(key, part):
    cells = nearest_sticks(key)
    freq_x = signed_frequency_drawn(cells // NG, NG)
    freq_y = signed_frequency_drawn(cells % NG, NG)
    depth = signed_frequency_drawn(jnp.arange(NG, dtype=jnp.int32), NG)
    squares = (freq_x * freq_x + freq_y * freq_y)[:, None] + (depth * depth)[None, :]
    return (squares <= RAD * RAD).astype(jnp.int32)


def levels(key, shape, pieces, smallest, top_value):
    def one(position, blocks):
        heights = jax.random.uniform(jax.random.fold_in(jax.random.fold_in(key, 6), position), (blocks,), jnp.float32, smallest / len(pieces), top_value / len(pieces))
        return jnp.repeat(jnp.exp(heights), shape[position] // blocks).reshape((-1,) + (1,) * (len(shape) - position - 1))

    factor_of = one(*pieces[0])
    for cut in pieces[1:]:
        factor_of = factor_of * one(*cut)
    return factor_of


def gaussian(key, dims, deviation, bound, split=(), kind=jnp.bfloat16):
    values = jax.random.normal(key, dims, jnp.float32) * deviation
    if len(split) > 0:
        values = levels(key, dims, split, -0.22, 0.18) * values
    return jnp.clip(values, min=-bound, max=bound).astype(kind)


def setup_inputs(seed: int = 0) -> dict:
    key_list = jax.random.split(jax.random.key(seed), 6)
    block = gaussian(key_list[0], (BLOCK, 2, NSTK, NG), 1.0, 6.0, ((0, 8), (2, 64)))
    bands = gaussian(key_list[1], (NB_ALL, 2, NSTK, NG), (NSTK * NG // 3) ** -0.5, 0.01953125, ((0, 8), (2, 64)))
    potential = jnp.clip(-4.0 + 5.0 * jax.random.uniform(key_list[2], (ZPAD, NG, NG), jnp.float32) ** levels(key_list[2], (ZPAD, NG, NG), ((0, 64),), -0.2, 0.2), -4.0, 1.0)
    stick_cells = draw_stick_cells(jax.random.fold_in(key_list[5], 71), 0)
    sphere_mask = draw_sphere_mask(jax.random.fold_in(key_list[5], 71), 0)
    return dict(block=block, bands=bands, potential=potential, stick_cells=stick_cells, sphere_mask=sphere_mask)


def signed_frequency(index, period):
    return jnp.where(index < period // 2, index, index - period)


def inner_products(left, right):
    left_rows = left.shape[0]
    right_rows = right.shape[0]
    turned = jnp.stack([right[:, 1], -right[:, 0]], axis=1)
    joined = jnp.concatenate([right, turned], axis=0).reshape(2 * right_rows, -1)
    result = jnp.dot(left.reshape(left_rows, -1), joined.T, preferred_element_type=jnp.float32)
    return jnp.transpose(result.reshape(left_rows, 2, right_rows), (1, 0, 2))


def reference(block, bands, potential, stick_cells, sphere_mask):
    column_x = stick_cells // NG
    column_y = stick_cells % NG
    freq_x = signed_frequency(column_x, NG)
    freq_y = signed_frequency(column_y, NG)
    depth = signed_frequency(jnp.arange(NG, dtype=jnp.int32), NG)
    squares = (freq_x * freq_x + freq_y * freq_y)[:, None] + (depth * depth)[None, :]
    kinetic = (2.0 / (RAD * RAD)) * squares.astype(jnp.float32)
    weights = sphere_mask.astype(jnp.float32)
    masked = block * sphere_mask.astype(jnp.bfloat16)[None, None]
    landscape = jnp.transpose(potential[:NG], (1, 2, 0))

    def apply_one(single):
        values = single.astype(jnp.float32)
        real_grid = jnp.zeros((NG, NG, NG), jnp.float32).at[column_x, column_y].set(values[0])
        imag_grid = jnp.zeros((NG, NG, NG), jnp.float32).at[column_x, column_y].set(values[1])
        field = jnp.fft.ifftn(lax.complex(real_grid, imag_grid))
        spectrum = jnp.fft.fftn(field * landscape)
        picked = spectrum[column_x, column_y]
        real_part = weights * (kinetic * values[0] + jnp.real(picked))
        imag_part = weights * (kinetic * values[1] + jnp.imag(picked))
        return jnp.stack([real_part, imag_part]).astype(jnp.bfloat16)

    applied = lax.map(apply_one, masked)
    correlation = inner_products(bands, masked)
    subspace = inner_products(bands, applied)
    return applied, correlation, subspace
```

```python
import jax
import jax.numpy as jnp
import ml_dtypes
import numpy as np
from jax import lax
from jax.experimental import pallas as pl
from jax.experimental.pallas import tpu as pltpu
from jax.sharding import PartitionSpec as P

NG = 128
RAD = 32
WIN = 64
GROUP = 4
RING = 16
BANDS = 2
STICKS = 160
ROWS = 48
ALL = STICKS * RING
F32 = jnp.float32
BF16 = jnp.bfloat16


def split_table(table):
    high = table.astype(ml_dtypes.bfloat16)
    low = (table - high.astype(np.float64)).astype(ml_dtypes.bfloat16)
    return high, low


def angle(first, second):
    return 2.0 * np.pi / NG * np.mod(np.outer(first, second), NG)


def depth_tables():
    k = np.arange(NG)
    theta = angle(np.arange(NG), k)
    inverse = np.zeros((RING, 2, 8, 2 * NG))
    theta = theta.reshape(RING, 8, NG)
    inverse[:, 0] = np.concatenate([np.cos(theta), -np.sin(theta)], axis=-1)
    inverse[:, 1] = np.concatenate([np.sin(theta), np.cos(theta)], axis=-1)
    forward = np.zeros((RING, 2, 8, 2 * NG))
    forward[:, 0] = np.concatenate([np.cos(theta), -np.sin(theta)], axis=-1)
    forward[:, 1] = np.concatenate([np.sin(theta), np.cos(theta)], axis=-1)
    return split_table(inverse.reshape(2 * NG, 2 * NG)), split_table(forward.reshape(2 * NG, 2 * NG))


def across_tables():
    y = np.arange(NG)
    j = np.arange(WIN)
    theta = angle(j, y)
    lower = np.sin(theta)
    lower[0] = np.where(y % 2 == 0, 1.0, -1.0)
    high, low = split_table(np.concatenate([np.cos(theta), lower], axis=0))
    stacked = np.concatenate([high, high, low, low], axis=0)
    wide = np.concatenate([high.T, low.T], axis=1)
    return stacked, wide


def down_tables():
    freq = np.arange(WIN) - RAD
    theta = angle(np.arange(NG), freq)
    cosine, sine = np.cos(theta) / NG**3, np.sin(theta) / NG**3
    inverse = np.block([[cosine, -sine], [sine, cosine]])
    cosine, sine = np.cos(theta).T, np.sin(theta).T
    forward = np.block([[cosine, sine], [-sine, cosine]])
    return split_table(inverse), split_table(forward)


def lane_order():
    order = np.concatenate([np.arange(WIN), [WIN], np.arange(NG - 1, WIN, -1)])
    matrix = np.zeros((NG, NG))
    matrix[order, np.arange(NG)] = 1.0
    return matrix.astype(ml_dtypes.bfloat16)


def split(value):
    high = value.astype(BF16)
    low = (value - high.astype(F32)).astype(BF16)
    return high, low


def dot(left, right, dims=((1,), (0,))):
    return lax.dot_general(left, right, (dims, ((), ())), preferred_element_type=F32)


def spread_kernel(part_ref, high_ref, low_ref, out_ref):
    for band in range(BANDS):
        real = part_ref[:, 2 * band].reshape(STICKS, NG)
        imag = part_ref[:, 2 * band + 1].reshape(STICKS, NG)
        both = jnp.concatenate([real, imag], axis=1)
        field = dot(high_ref[...], both, ((1,), (1,))) + dot(low_ref[...], both, ((1,), (1,)))
        out_ref[:, 16 * band : 16 * band + 16, :] = field[:, :NG].reshape(RING, 16, NG)
        rest = field[:, NG:].reshape(RING, 2, 8, STICKS - NG)
        for part in range(2):
            g = 2 * band + part
            out_ref[:, 32:40, 32 * g : 32 * g + 32] = rest[:, part]
    cells = part_ref[:, 2 * BANDS].reshape(STICKS, NG)
    lane = lax.broadcasted_iota(jnp.int32, (8, NG), 1)
    row = lax.broadcasted_iota(jnp.int32, (8, NG), 0)
    pick = jnp.where(row < 1, jnp.where(lane == 0, 128.0, jnp.where(lane == 1, 1.0, 0.0)), 0.0)
    flat = dot(pick.astype(BF16), cells, ((1,), (1,)))
    tail = jnp.concatenate([flat[0:1, NG:], jnp.zeros((1, 2 * NG - STICKS), F32)], axis=1)
    index = lax.broadcasted_iota(jnp.int32, (8, NG), 0)
    block = jnp.where(index == 0, flat[0:1, :NG], jnp.where(index == 1, tail, 0.0))
    out_ref[:, 40:48, :] = jnp.broadcast_to(block[None], (RING, 8, NG))


def plane_kernel(
    recv_ref, v_ref, stack_ref, wide_ref, xa_ref, xh_ref, fh_ref, fl_ref, order_ref,
    out_ref, val_ref, low_ref, cell_ref, onehot_ref, tall_ref, flat_ref, left_ref, mid_ref, lift_ref,
):
    for src in range(RING):
        val_ref[:, src * NG : (src + 1) * NG] = recv_ref[src, 0:32, :]
        cell_ref[:, src * NG : (src + 1) * NG] = jnp.broadcast_to(recv_ref[src, 40:41, :], (8, NG))
        start = RING * NG + 32 * src
        for g in range(4):
            val_ref[8 * g : 8 * g + 8, start : start + 32] = recv_ref[src, 32:40, 32 * g : 32 * g + 32]
        cell_ref[:, start : start + 32] = jnp.broadcast_to(recv_ref[src, 41:42, 0:32], (8, 32))

    cells = cell_ref[...].astype(jnp.int32)
    x_index = jnp.bitwise_and(lax.shift_right_logical(cells, 7) + RAD, NG - 1)
    y_index = jnp.bitwise_and(cells, NG - 1)
    x_row, y_row = x_index[0:1], y_index[0:1]
    onehot_ref[...] = jnp.where(
        lax.broadcasted_iota(jnp.int32, (WIN, ALL), 0) == x_row, 1.0, 0.0
    ).astype(BF16)
    pick_y = jnp.where(lax.broadcasted_iota(jnp.int32, (NG, ALL), 0) == y_row, 1.0, 0.0).astype(BF16)
    flat_ref[...] = dot(stack_ref[...], pick_y).astype(BF16)
    tall_ref[...] = dot(pick_y, wide_ref[...], ((0,), (0,))).astype(BF16)

    rounded = val_ref[...].astype(BF16).astype(F32)
    low_ref[...] = val_ref[...] - rounded
    val_ref[...] = rounded

    lane = lax.broadcasted_iota(jnp.int32, (WIN, NG), 1)
    first = jnp.bitwise_and(lane, WIN - 1) == 0
    lower = lane < WIN

    @pl.loop(0, 8)
    def _(z):
        for g in range(4):
            for part, ref in enumerate((val_ref, low_ref)):
                row = ref[pl.ds(8 * g + z, 1), :]
                spread = jnp.broadcast_to(row, (WIN, ALL)).astype(BF16)
                at = (2 * g + part) * WIN
                left_ref[at : at + WIN, :] = spread * onehot_ref[...]
        full = dot(left_ref[...], tall_ref[...])
        full = full[:, :NG] + full[:, NG:]
        parts = [full[2 * g * WIN : (2 * g + 1) * WIN] + full[(2 * g + 1) * WIN : (2 * g + 2) * WIN] for g in range(4)]
        for band in range(BANDS):
            real, imag = parts[2 * band], parts[2 * band + 1]
            real_turn, imag_turn = pltpu.roll(real, WIN, 1), pltpu.roll(imag, WIN, 1)
            new_real = jnp.where(first, real, jnp.where(lower, real - imag_turn, real_turn + imag))
            new_imag = jnp.where(first, imag, jnp.where(lower, imag + real_turn, imag_turn - real))
            mid_ref[z, 0:WIN, band * NG : (band + 1) * NG] = new_real
            mid_ref[z, WIN:, band * NG : (band + 1) * NG] = new_imag

    for owner in range(GROUP):
        for i in range(2):
            z = 2 * owner + i
            potential = dot(v_ref[owner, 0, i], order_ref[...]) + dot(v_ref[owner, 1, i], order_ref[...])
            high, low = split(mid_ref[z])
            field = dot(xa_ref[...], jnp.concatenate([high, high], axis=0)) + dot(xh_ref[...], low)
            wide = jnp.concatenate([potential, potential], axis=1)
            weighted = field * jnp.concatenate([wide, wide], axis=0)
            high, low = split(weighted)
            folded = dot(fh_ref[...], high) + dot(fh_ref[...], low) + dot(fl_ref[...], high)
            for band in range(BANDS):
                real = folded[:WIN, band * NG : (band + 1) * NG]
                imag = folded[WIN:, band * NG : (band + 1) * NG]
                real_turn, imag_turn = pltpu.roll(real, WIN, 1), pltpu.roll(imag, WIN, 1)
                left_real = jnp.where(first, real, jnp.where(lower, real + real_turn, imag_turn - imag))
                left_imag = jnp.where(first, imag, jnp.where(lower, imag + imag_turn, real - real_turn))
                for part, value in enumerate((left_real, left_imag)):
                    high, low = split(value)
                    lift_ref[2 * band + part, z, :, 0:NG] = high
                    lift_ref[2 * band + part, z, :, NG:] = low

    @pl.loop(0, ALL // 256)
    def _(t):
        cols = pl.ds(pl.multiple_of(t * 256, 256), 256)
        select = onehot_ref[:, cols].astype(F32)[None]
        for g in range(4):
            rows = lift_ref[g].reshape(8 * WIN, 2 * NG)
            full = dot(rows, flat_ref[0:256, cols]) + dot(rows, flat_ref[256:512, cols])
            val_ref[8 * g : 8 * g + 8, cols] = jnp.sum(full.reshape(8, WIN, 256) * select, axis=1)

    for src in range(RING):
        out_ref[src, 0:32, :] = val_ref[:, src * NG : (src + 1) * NG]
        start = RING * NG + 32 * src
        for g in range(4):
            out_ref[src, 32:40, 32 * g : 32 * g + 32] = val_ref[8 * g : 8 * g + 8, start : start + 32]
        out_ref[src, 40:48, :] = jnp.zeros((8, NG), F32)


def finish_kernel(recv_ref, part_ref, high_ref, low_ref, out_ref, copies_ref, line_ref, pack_ref):
    squares = part_ref[:, 2 * BANDS].reshape(STICKS, NG).astype(F32)
    signed = jnp.where(squares < NG // 2, squares, squares - NG)
    across = signed * signed
    across = across[:, 0:1] + across[:, 1:2]
    k = lax.broadcasted_iota(jnp.int32, (STICKS, NG), 1)
    k = jnp.where(k < NG // 2, k, k - NG)
    total = across + (k * k).astype(F32)
    weight = jnp.where(total <= RAD * RAD, 1.0, 0.0)
    kinetic = 2.0 / (RAD * RAD) * total
    for band in range(BANDS):
        line_ref[:, 0:NG] = recv_ref[:, 16 * band : 16 * band + 16, :].reshape(2 * NG, NG)
        for src in range(RING):
            for part in range(2):
                g = 2 * band + part
                at = 16 * src + 8 * part
                line_ref[at : at + 8, NG : NG + 32] = recv_ref[src, 32:40, 32 * g : 32 * g + 32]
        high, low = split(jnp.transpose(line_ref[...])[:STICKS])
        product = dot(high, high_ref[...]) + dot(low, high_ref[...]) + dot(high, low_ref[...])
        for part in range(2):
            masked = part_ref[:, 2 * band + part].reshape(STICKS, NG).astype(F32)
            value = weight * (kinetic * masked + product[:, part * NG : (part + 1) * NG])
            value = value.reshape(GROUP, STICKS // GROUP, NG)
            out_ref[:, 2 * band + part] = value.astype(BF16)
            half = STICKS // GROUP // 2
            for src in range(GROUP):
                at = ((2 * band + part) * GROUP + src) * half
                turned = pltpu.roll(value[src, half:], NG // 2, 1)
                pack_ref[at : at + half, :] = value[src, :half] + turned
    packed = pack_ref[...].astype(BF16)
    for copy in range(copies_ref.shape[0]):
        copies_ref[copy] = packed


def vmem_call(kernel, out_shape, inputs, scratch=()):
    vmem = pl.BlockSpec(memory_space=pltpu.VMEM)
    return pl.pallas_call(
        kernel,
        out_shape=out_shape,
        in_specs=[vmem] * len(inputs),
        out_specs=jax.tree.map(lambda _: vmem, out_shape),
        scratch_shapes=list(scratch),
        compiler_params=pltpu.CompilerParams(vmem_limit_bytes=56 * 1024 * 1024),
    )(*inputs)


def spread(part):
    (high, low), _ = depth_tables()
    shape = jax.ShapeDtypeStruct((RING, ROWS, NG), F32)
    return vmem_call(spread_kernel, shape, (part, high, low))


def planes(recv, potentials):
    stack, wide = across_tables()
    (xh, xl), (fh, fl) = down_tables()
    xa = np.concatenate([xh, xl], axis=1)
    shape = jax.ShapeDtypeStruct((RING, ROWS, NG), F32)
    scratch = (
        pltpu.VMEM((32, ALL), F32),
        pltpu.VMEM((32, ALL), F32),
        pltpu.VMEM((8, ALL), F32),
        pltpu.VMEM((WIN, ALL), BF16),
        pltpu.VMEM((ALL, 2 * NG), BF16),
        pltpu.VMEM((4 * NG, ALL), BF16),
        pltpu.VMEM((8 * WIN, ALL), BF16),
        pltpu.VMEM((8, 2 * WIN, 2 * NG), F32),
        pltpu.VMEM((4, 8, WIN, 2 * NG), BF16),
    )
    inputs = (recv, potentials, stack, wide, xa, xh, fh, fl, lane_order())
    return vmem_call(plane_kernel, shape, inputs, scratch)


def finish(recv, part, copies):
    _, (high, low) = depth_tables()
    rows = BANDS * STICKS
    shape = (
        jax.ShapeDtypeStruct((GROUP, 2 * BANDS, STICKS // GROUP, NG), BF16),
        jax.ShapeDtypeStruct((copies, rows, NG), BF16),
    )
    scratch = (pltpu.VMEM((2 * NG, 2 * NG), F32), pltpu.VMEM((rows, NG), F32))
    return vmem_call(finish_kernel, shape, (recv, part, high, low), scratch)


def pack(value):
    half = value.shape[2] // 2
    return value[:, :, :half] + jnp.roll(value[:, :, half:], NG // 2, axis=3)


def pairing(bands, vectors):
    full = lax.dot_general(
        bands, vectors, (((0, 3, 4), (3, 4, 5)), ((), ())), preferred_element_type=F32
    )
    real = full[:, 0, :, :, 0] + full[:, 1, :, :, 1]
    imag = full[:, 0, :, :, 1] - full[:, 1, :, :, 0]
    return jnp.stack([real, imag])


def exchange(value, axis, groups=None):
    return lax.all_to_all(value, axis, 0, 0, axis_index_groups=groups, tiled=True)


def to_all(value, axis, count, groups=None):
    return exchange(jnp.broadcast_to(value[None], (count, *value.shape)), axis, groups)


def per_device(block, bands, potential, stick_cells, sphere_mask):
    size = lax.axis_size("pw")
    teams = lax.axis_size("band")
    own, sticks, rows = block.shape[0], block.shape[2], bands.shape[0]
    fours = [[i * GROUP + j for j in range(GROUP)] for i in range(size // GROUP)]
    rings = [[i * GROUP + j for i in range(size // GROUP)] for j in range(GROUP)]

    inside = sphere_mask.astype(BF16)[None, None]
    masked = block * inside
    lane = jnp.arange(NG, dtype=jnp.int32)[None, :]
    column = jnp.where(lane == 0, stick_cells[:, None] // NG, jnp.where(lane == 1, stick_cells[:, None] % NG, 0))
    grouped = masked.reshape(GROUP, 2 * BANDS, sticks, NG)
    column = jnp.broadcast_to(column.astype(BF16)[None, None], (GROUP, 1, sticks, NG))
    part = exchange(jnp.concatenate([grouped, column], axis=1), "pw", fours)
    sent = spread(part)
    recv = exchange(sent, "pw", rings)

    bands_rows = pack(bands * inside).reshape(-1, NG)
    v_high = lax.reduce_precision(potential, 8, 7)
    v_low = (potential - v_high).astype(BF16)
    potential_rows = jnp.stack([v_high.astype(BF16), v_low]).reshape(-1, NG)
    side = to_all(jnp.concatenate([bands_rows, potential_rows], axis=0), "pw", GROUP, fours)
    split_at = bands_rows.shape[0]
    bands_all = side[:, :split_at].reshape(GROUP, rows, 2, sticks // 2, NG)
    potentials = side[:, split_at:].reshape(GROUP, 2, potential.shape[0], NG, NG)
    shape = (teams, BANDS, 2, GROUP, sticks // 2, NG)
    packed = jnp.transpose(pack(part[:, : 2 * BANDS]), (1, 0, 2, 3)).reshape(-1, NG)
    masked_all = to_all(packed, "band", teams).reshape(shape)

    back = exchange(planes(recv, potentials), "pw", rings)
    result, copies = finish(back, part, teams)
    applied_all = exchange(copies, "band").reshape(shape)
    applied = exchange(result, "pw", fours).reshape(own, 2, sticks, NG)

    terms = jnp.stack([pairing(bands_all, masked_all), pairing(bands_all, applied_all)])
    total = jnp.sum(to_all(terms.reshape(-1, NG), "pw", size // GROUP, rings), axis=0)
    total = to_all(total, "pw", GROUP, fours).reshape(GROUP, 2, 2, rows, teams, BANDS)
    total = jnp.transpose(total, (1, 2, 3, 4, 0, 5)).reshape(2, 2, rows, teams * own)
    return (applied, total[0], total[1])


def solution(mesh):
    return jax.shard_map(
        per_device,
        mesh=mesh,
        in_specs=(
            P("band", None, "pw", None),
            P("band", None, "pw", None),
            P("pw", None, None),
            P("pw"),
            P("pw", None),
        ),
        out_specs=(P("band", None, "pw", None), P(None, "band", None), P(None, "band", None)),
        check_vma=False,
    )
```

```python
import jax
import jax.numpy as jnp
import ml_dtypes
import numpy as np
from jax import lax
from jax.experimental import pallas as pl
from jax.experimental.pallas import tpu as pltpu
from jax.sharding import PartitionSpec as P

NG = 128
RAD = 32
WIN = 64
GROUP = 4
RING = 16
BANDS = 2
STICKS = 160
ROWS = 48
ALL = STICKS * RING
F32 = jnp.float32
BF16 = jnp.bfloat16


def split_table(table):
    high = table.astype(ml_dtypes.bfloat16)
    low = (table - high.astype(np.float64)).astype(ml_dtypes.bfloat16)
    return high, low


def angle(first, second):
    return 2.0 * np.pi / NG * np.mod(np.outer(first, second), NG)


def depth_tables():
    k = np.arange(NG)
    theta = angle(np.arange(NG), k)
    inverse = np.zeros((RING, 2, 8, 2 * NG))
    theta = theta.reshape(RING, 8, NG)
    inverse[:, 0] = np.concatenate([np.cos(theta), -np.sin(theta)], axis=-1)
    inverse[:, 1] = np.concatenate([np.sin(theta), np.cos(theta)], axis=-1)
    forward = np.zeros((RING, 2, 8, 2 * NG))
    forward[:, 0] = np.concatenate([np.cos(theta), -np.sin(theta)], axis=-1)
    forward[:, 1] = np.concatenate([np.sin(theta), np.cos(theta)], axis=-1)
    return split_table(inverse.reshape(2 * NG, 2 * NG)), split_table(forward.reshape(2 * NG, 2 * NG))


def across_tables():
    y = np.arange(NG)
    j = np.arange(WIN)
    theta = angle(j, y)
    lower = np.sin(theta)
    lower[0] = np.where(y % 2 == 0, 1.0, -1.0)
    high, low = split_table(np.concatenate([np.cos(theta), lower], axis=0))
    stacked = np.concatenate([high, high, low, low], axis=0)
    wide = np.concatenate([high.T, low.T], axis=1)
    return stacked, wide


def down_tables():
    freq = np.arange(WIN) - RAD
    theta = angle(np.arange(NG), freq)
    cosine, sine = np.cos(theta) / NG**3, np.sin(theta) / NG**3
    inverse = np.block([[cosine, -sine], [sine, cosine]])
    cosine, sine = np.cos(theta).T, np.sin(theta).T
    forward = np.block([[cosine, sine], [-sine, cosine]])
    return split_table(inverse), split_table(forward)


def lane_order():
    order = np.concatenate([np.arange(WIN), [WIN], np.arange(NG - 1, WIN, -1)])
    matrix = np.zeros((NG, NG))
    matrix[order, np.arange(NG)] = 1.0
    return matrix.astype(ml_dtypes.bfloat16)


def split(value):
    high = value.astype(BF16)
    low = (value - high.astype(F32)).astype(BF16)
    return high, low


def dot(left, right, dims=((1,), (0,))):
    return lax.dot_general(left, right, (dims, ((), ())), preferred_element_type=F32)


def exponent(peak):
    return jnp.ceil(jnp.log2(jnp.maximum(peak, 1e-30)))


def encode_scale(power):
    return jnp.exp2(15.0 - power) * 0.999


def decode_scale(power):
    return jnp.exp2(power - 15.0) * (1.0 / 0.999)


def to_short(value):
    return jnp.floor(value + 0.5).astype(jnp.int32).astype(jnp.int16)


def from_short(value):
    return value.astype(jnp.int32).astype(F32)


def spread_kernel(part_ref, high_ref, low_ref, out_ref):
    powers, tails = [], []
    for band in range(BANDS):
        real = part_ref[:, 2 * band].reshape(STICKS, NG)
        imag = part_ref[:, 2 * band + 1].reshape(STICKS, NG)
        both = jnp.concatenate([real, imag], axis=1)
        field = dot(high_ref[...], both, ((1,), (1,))) + dot(low_ref[...], both, ((1,), (1,)))
        power = exponent(jnp.max(jnp.abs(field), axis=0, keepdims=True))
        field = field * encode_scale(power)
        out_ref[:, 16 * band : 16 * band + 16, :] = to_short(field[:, :NG]).reshape(RING, 16, NG)
        rest = field[:, NG:].reshape(RING, 2, 8, STICKS - NG)
        tails += [rest[:, 0], rest[:, 1]]
        powers.append(power)
    cells = part_ref[:, 2 * BANDS].reshape(STICKS, NG)
    lane = lax.broadcasted_iota(jnp.int32, (8, NG), 1)
    pick = jnp.where(lane == 0, 128.0, jnp.where(lane == 1, 1.0, 0.0))
    flat = dot(pick.astype(BF16), cells, ((1,), (1,)))[0:1]
    index = lax.broadcasted_iota(jnp.int32, (8, NG), 0)
    notes = jnp.zeros((8, NG), F32)
    for place, line in enumerate((flat, *powers)):
        tail = jnp.concatenate([line[:, NG:], jnp.zeros((1, 2 * NG - STICKS), F32)], axis=1)
        notes = jnp.where(index == 2 * place, line[:, :NG], jnp.where(index == 2 * place + 1, tail, notes))
    notes = jnp.broadcast_to(notes[None], (RING, 8, NG))
    last = jnp.concatenate([jnp.concatenate(tails, axis=2), notes], axis=1)
    out_ref[:, 32:48, :] = to_short(last)


def plane_kernel(
    me_ref, recv_ref, v0_ref, v1_ref, v2_ref, v3_ref, stack_ref, wide_ref, xa_ref, xh_ref, fh_ref, fl_ref, order_ref,
    out_ref, val_ref, low_ref, cell_ref, onehot_ref, tall_ref, flat_ref, left_ref, mid_ref, lift_ref, tail_ref,
):
    for src in range(RING):
        val_ref[:, src * NG : (src + 1) * NG] = from_short(recv_ref[src, 0:32, :])
        last = from_short(recv_ref[src, 32:48, :])
        start = RING * NG + 32 * src
        for g in range(4):
            val_ref[8 * g : 8 * g + 8, start : start + 32] = last[:8, 32 * g : 32 * g + 32]
        for place in range(3):
            cell_ref[place : place + 1, src * NG : (src + 1) * NG] = last[8 + 2 * place : 9 + 2 * place]
            cell_ref[place : place + 1, start : start + 32] = last[9 + 2 * place : 10 + 2 * place, 0:32]

    cells = cell_ref[0:1, :].astype(jnp.int32)
    x_index = jnp.bitwise_and(lax.shift_right_logical(cells, 7) + RAD, NG - 1)
    y_index = jnp.bitwise_and(cells, NG - 1)
    onehot_ref[...] = jnp.where(
        lax.broadcasted_iota(jnp.int32, (WIN, ALL), 0) == x_index, 1.0, 0.0
    ).astype(BF16)
    pick_y = jnp.where(lax.broadcasted_iota(jnp.int32, (NG, ALL), 0) == y_index, 1.0, 0.0).astype(BF16)
    flat_ref[...] = dot(stack_ref[...], pick_y).astype(BF16)
    tall_ref[...] = dot(pick_y, wide_ref[...], ((0,), (0,))).astype(BF16)

    for band in range(BANDS):
        half = slice(16 * band, 16 * band + 16)
        value = val_ref[half, :] * decode_scale(cell_ref[1 + band : 2 + band, :])
        rounded = value.astype(BF16).astype(F32)
        low_ref[half, :] = value - rounded
        val_ref[half, :] = rounded

    lane = lax.broadcasted_iota(jnp.int32, (WIN, NG), 1)
    first = jnp.bitwise_and(lane, WIN - 1) == 0
    lower = lane < WIN

    @pl.loop(0, 8)
    def _(z):
        for g in range(4):
            for part, ref in enumerate((val_ref, low_ref)):
                row = ref[pl.ds(8 * g + z, 1), :]
                spread = jnp.broadcast_to(row, (16, ALL)).astype(BF16)
                spread = jnp.concatenate([spread] * (WIN // 16), axis=0)
                at = (2 * g + part) * WIN
                left_ref[at : at + WIN, :] = spread * onehot_ref[...]
        full = dot(left_ref[...], tall_ref[...])
        full = full[:, :NG] + full[:, NG:]
        parts = [full[2 * g * WIN : (2 * g + 1) * WIN] + full[(2 * g + 1) * WIN : (2 * g + 2) * WIN] for g in range(4)]
        for band in range(BANDS):
            real, imag = parts[2 * band], parts[2 * band + 1]
            real_turn, imag_turn = pltpu.roll(real, WIN, 1), pltpu.roll(imag, WIN, 1)
            new_real = jnp.where(first, real, jnp.where(lower, real - imag_turn, real_turn + imag))
            new_imag = jnp.where(first, imag, jnp.where(lower, imag + real_turn, imag_turn - real))
            mid_ref[z, 0:WIN, band * NG : (band + 1) * NG] = new_real
            mid_ref[z, WIN:, band * NG : (band + 1) * NG] = new_imag

    me = me_ref[0]
    for turn, v_ref in enumerate((v0_ref, v1_ref, v2_ref, v3_ref)):
        for i in range(2):
            z = 2 * jnp.bitwise_xor(me, turn) + i
            potential = dot(v_ref[0, i], order_ref[...]) + dot(v_ref[1, i], order_ref[...])
            high, low = split(mid_ref[z])
            field = dot(xa_ref[...], jnp.concatenate([high, high], axis=0)) + dot(xh_ref[...], low)
            wide = jnp.concatenate([potential, potential], axis=1)
            weighted = field * jnp.concatenate([wide, wide], axis=0)
            high, low = split(weighted)
            folded = dot(fh_ref[...], high) + dot(fh_ref[...], low) + dot(fl_ref[...], high)
            for band in range(BANDS):
                real = folded[:WIN, band * NG : (band + 1) * NG]
                imag = folded[WIN:, band * NG : (band + 1) * NG]
                real_turn, imag_turn = pltpu.roll(real, WIN, 1), pltpu.roll(imag, WIN, 1)
                left_real = jnp.where(first, real, jnp.where(lower, real + real_turn, imag_turn - imag))
                left_imag = jnp.where(first, imag, jnp.where(lower, imag + imag_turn, real - real_turn))
                for part, value in enumerate((left_real, left_imag)):
                    high, low = split(value)
                    lift_ref[2 * band + part, z, :, 0:NG] = high
                    lift_ref[2 * band + part, z, :, NG:] = low

    @pl.loop(0, ALL // 256)
    def _(t):
        cols = pl.ds(pl.multiple_of(t * 256, 256), 256)
        select = onehot_ref[:, cols].astype(F32)[None]
        for g in range(4):
            rows = lift_ref[g].reshape(8 * WIN, 2 * NG)
            full = dot(rows, flat_ref[0:256, cols]) + dot(rows, flat_ref[256:512, cols])
            val_ref[8 * g : 8 * g + 8, cols] = jnp.sum(full.reshape(8, WIN, 256) * select, axis=1)

    for band in range(BANDS):
        half = slice(16 * band, 16 * band + 16)
        power = exponent(jnp.max(jnp.abs(val_ref[half, :]), axis=0, keepdims=True))
        cell_ref[1 + band : 2 + band, :] = power
        val_ref[half, :] = val_ref[half, :] * encode_scale(power)
    tail_ref[...] = jnp.zeros((RING, 16, NG), F32)
    for src in range(RING):
        out_ref[src, 0:32, :] = to_short(val_ref[:, src * NG : (src + 1) * NG])
        start = RING * NG + 32 * src
        for g in range(4):
            tail_ref[src, 0:8, 32 * g : 32 * g + 32] = val_ref[8 * g : 8 * g + 8, start : start + 32]
        for place in range(1, 3):
            tail_ref[src, 8 + 2 * place : 9 + 2 * place, :] = cell_ref[place : place + 1, src * NG : (src + 1) * NG]
            tail_ref[src, 9 + 2 * place : 10 + 2 * place, 0:32] = cell_ref[place : place + 1, start : start + 32]
    out_ref[:, 32:48, :] = to_short(tail_ref[...])


def finish_kernel(recv_ref, part_ref, high_ref, low_ref, out_ref, copies_ref, line_ref, pack_ref):
    squares = part_ref[:, 2 * BANDS].reshape(STICKS, NG).astype(F32)
    signed = jnp.where(squares < NG // 2, squares, squares - NG)
    across = signed * signed
    across = across[:, 0:1] + across[:, 1:2]
    k = lax.broadcasted_iota(jnp.int32, (STICKS, NG), 1)
    k = jnp.where(k < NG // 2, k, k - NG)
    total = across + (k * k).astype(F32)
    weight = jnp.where(total <= RAD * RAD, 1.0, 0.0)
    kinetic = 2.0 / (RAD * RAD) * total
    for band in range(BANDS):
        for src in range(RING):
            last = from_short(recv_ref[src, 32:48, :])
            main = from_short(recv_ref[src, 16 * band : 16 * band + 16, :])
            scale = decode_scale(last[10 + 2 * band : 12 + 2 * band])
            line_ref[16 * src : 16 * src + 16, 0:NG] = main * scale[0:1]
            for part in range(2):
                g = 2 * band + part
                at = 16 * src + 8 * part
                line_ref[at : at + 8, NG : NG + 32] = last[:8, 32 * g : 32 * g + 32] * scale[1:2, 0:32]
        high, low = split(jnp.transpose(line_ref[...])[:STICKS])
        product = dot(high, high_ref[...]) + dot(low, high_ref[...]) + dot(high, low_ref[...])
        for part in range(2):
            masked = part_ref[:, 2 * band + part].reshape(STICKS, NG).astype(F32)
            value = weight * (kinetic * masked + product[:, part * NG : (part + 1) * NG])
            value = value.reshape(GROUP, STICKS // GROUP, NG)
            out_ref[:, 2 * band + part] = value.astype(BF16)
            half = STICKS // GROUP // 2
            for src in range(GROUP):
                at = ((2 * band + part) * GROUP + src) * half
                turned = pltpu.roll(value[src, half:], NG // 2, 1)
                pack_ref[at : at + half, :] = value[src, :half] + turned
    packed = pack_ref[...].astype(BF16)
    for copy in range(copies_ref.shape[0]):
        copies_ref[copy] = packed


def vmem_call(kernel, out_shape, inputs, scratch=(), scalars=0):
    vmem = pl.BlockSpec(memory_space=pltpu.VMEM)
    smem = pl.BlockSpec(memory_space=pltpu.SMEM)
    return pl.pallas_call(
        kernel,
        out_shape=out_shape,
        in_specs=[smem] * scalars + [vmem] * (len(inputs) - scalars),
        out_specs=jax.tree.map(lambda _: vmem, out_shape),
        scratch_shapes=list(scratch),
        compiler_params=pltpu.CompilerParams(vmem_limit_bytes=56 * 1024 * 1024),
    )(*inputs)


def spread(part):
    (high, low), _ = depth_tables()
    shape = jax.ShapeDtypeStruct((RING, ROWS, NG), jnp.int16)
    return vmem_call(spread_kernel, shape, (part, high, low))


def planes(me, recv, potentials):
    stack, wide = across_tables()
    (xh, xl), (fh, fl) = down_tables()
    xa = np.concatenate([xh, xl], axis=1)
    shape = jax.ShapeDtypeStruct((RING, ROWS, NG), jnp.int16)
    scratch = (
        pltpu.VMEM((32, ALL), F32),
        pltpu.VMEM((32, ALL), F32),
        pltpu.VMEM((8, ALL), F32),
        pltpu.VMEM((WIN, ALL), BF16),
        pltpu.VMEM((ALL, 2 * NG), BF16),
        pltpu.VMEM((4 * NG, ALL), BF16),
        pltpu.VMEM((8 * WIN, ALL), BF16),
        pltpu.VMEM((8, 2 * WIN, 2 * NG), F32),
        pltpu.VMEM((4, 8, WIN, 2 * NG), BF16),
        pltpu.VMEM((RING, 16, NG), F32),
    )
    inputs = (me, recv, *potentials, stack, wide, xa, xh, fh, fl, lane_order())
    return vmem_call(plane_kernel, shape, inputs, scratch, 1)


def finish(recv, part, copies):
    _, (high, low) = depth_tables()
    rows = BANDS * STICKS
    shape = (
        jax.ShapeDtypeStruct((GROUP, 2 * BANDS, STICKS // GROUP, NG), BF16),
        jax.ShapeDtypeStruct((copies, rows, NG), BF16),
    )
    scratch = (pltpu.VMEM((2 * NG, 2 * NG), F32), pltpu.VMEM((rows, NG), F32))
    return vmem_call(finish_kernel, shape, (recv, part, high, low), scratch)


def pack(value):
    half = value.shape[2] // 2
    return value[:, :, :half] + jnp.roll(value[:, :, half:], NG // 2, axis=3)


def pairing(bands, vectors, labels):
    full = jnp.einsum("snprl," + labels + "->npgbq", bands, vectors, preferred_element_type=F32)
    real = full[:, 0, :, :, 0] + full[:, 1, :, :, 1]
    imag = full[:, 0, :, :, 1] - full[:, 1, :, :, 0]
    return jnp.stack([real, imag])


def partner(value, turn, size):
    return lax.ppermute(value, "pw", [(i, i ^ turn) for i in range(size)])


def place(pieces, me):
    result = jnp.zeros((GROUP, *pieces[0].shape), pieces[0].dtype)
    for turn, piece in enumerate(pieces):
        result = lax.dynamic_update_index_in_dim(result, piece, jnp.bitwise_xor(me, turn), 0)
    return result


def exchange(value, axis, groups=None):
    return lax.all_to_all(value, axis, 0, 0, axis_index_groups=groups, tiled=True)


def to_all(value, axis, count, groups=None):
    return exchange(jnp.broadcast_to(value[None], (count, *value.shape)), axis, groups)


def per_device(block, bands, potential, stick_cells, sphere_mask):
    size = lax.axis_size("pw")
    teams = lax.axis_size("band")
    me = jnp.bitwise_and(lax.axis_index("pw"), GROUP - 1)
    own, sticks, rows = block.shape[0], block.shape[2], bands.shape[0]
    fours = [[i * GROUP + j for j in range(GROUP)] for i in range(size // GROUP)]
    rings = [[i * GROUP + j for i in range(size // GROUP)] for j in range(GROUP)]

    inside = sphere_mask.astype(BF16)[None, None]
    masked = block * inside
    lane = jnp.arange(NG, dtype=jnp.int32)[None, :]
    column = jnp.where(lane == 0, stick_cells[:, None] // NG, jnp.where(lane == 1, stick_cells[:, None] % NG, 0))
    grouped = masked.reshape(GROUP, 2 * BANDS, sticks, NG)
    column = jnp.broadcast_to(column.astype(BF16)[None, None], (GROUP, 1, sticks, NG))
    part = exchange(jnp.concatenate([grouped, column], axis=1), "pw", fours)
    sent = spread(part)
    recv = exchange(sent, "pw", rings)

    bands_rows = pack(bands * inside).reshape(-1, NG)
    v_high = lax.reduce_precision(potential, 8, 7)
    v_low = (potential - v_high).astype(BF16)
    potential_rows = jnp.stack([v_high.astype(BF16), v_low]).reshape(-1, NG)
    side = jnp.concatenate([bands_rows, potential_rows], axis=0)
    sides = [side] + [partner(side, turn, size) for turn in range(1, GROUP)]
    split_at = bands_rows.shape[0]
    bands_all = place([piece[:split_at] for piece in sides], me).reshape(GROUP, rows, 2, sticks // 2, NG)
    potentials = [piece[split_at:].reshape(2, potential.shape[0], NG, NG) for piece in sides]
    vectors = part[:, : 2 * BANDS].reshape(GROUP * BANDS, 2, sticks, NG)
    masked_all = lax.all_gather(jnp.stack([vectors, vectors]), "band", axis=1, tiled=True)[0]
    masked_all = pack(masked_all.reshape(teams * GROUP * BANDS, 2, sticks, NG))
    masked_all = masked_all.reshape(teams, GROUP, BANDS, 2, sticks // 2, NG)

    back = exchange(planes(me.reshape(1), recv, potentials), "pw", rings)
    result, copies = finish(back, part, teams)
    applied_all = exchange(copies, "band").reshape(teams, BANDS, 2, GROUP, sticks // 2, NG)
    pieces = [lax.dynamic_index_in_dim(result, jnp.bitwise_xor(me, turn), 0, False) for turn in range(GROUP)]
    pieces = pieces[:1] + [partner(pieces[turn], turn, size) for turn in range(1, GROUP)]
    applied = place(pieces, me).reshape(own, 2, sticks, NG)

    terms = jnp.stack(
        [pairing(bands_all, masked_all, "gsbqrl"), pairing(bands_all, applied_all, "gbqsrl")]
    )
    total = jnp.sum(to_all(terms.reshape(-1, NG), "pw", size // GROUP, rings), axis=0)
    total = to_all(total, "pw", GROUP, fours).reshape(GROUP, 2, 2, rows, teams, BANDS)
    total = jnp.transpose(total, (1, 2, 3, 4, 0, 5)).reshape(2, 2, rows, teams * own)
    return (applied, total[0], total[1])


def solution(mesh):
    return jax.shard_map(
        per_device,
        mesh=mesh,
        in_specs=(
            P("band", None, "pw", None),
            P("band", None, "pw", None),
            P("pw", None, None),
            P("pw"),
            P("pw", None),
        ),
        out_specs=(P("band", None, "pw", None), P(None, "band", None), P(None, "band", None)),
        check_vma=False,
    )
```

```python
import jax
import jax.numpy as jnp
import ml_dtypes
import numpy as np
from jax import lax
from jax.experimental import pallas as pl
from jax.experimental.pallas import tpu as pltpu
from jax.sharding import PartitionSpec as P

NG = 128
RAD = 32
WIN = 64
GROUP = 4
RING = 16
BANDS = 2
STICKS = 160
ROWS = 48
ALL = STICKS * RING
F32 = jnp.float32
BF16 = jnp.bfloat16


def split_table(table):
    high = table.astype(ml_dtypes.bfloat16)
    low = (table - high.astype(np.float64)).astype(ml_dtypes.bfloat16)
    return high, low


def angle(first, second):
    return 2.0 * np.pi / NG * np.mod(np.outer(first, second), NG)


def depth_tables():
    k = np.arange(NG)
    theta = angle(np.arange(NG), k)
    inverse = np.zeros((RING, 2, 8, 2 * NG))
    theta = theta.reshape(RING, 8, NG)
    inverse[:, 0] = np.concatenate([np.cos(theta), -np.sin(theta)], axis=-1)
    inverse[:, 1] = np.concatenate([np.sin(theta), np.cos(theta)], axis=-1)
    forward = np.zeros((RING, 2, 8, 2 * NG))
    forward[:, 0] = np.concatenate([np.cos(theta), -np.sin(theta)], axis=-1)
    forward[:, 1] = np.concatenate([np.sin(theta), np.cos(theta)], axis=-1)
    return split_table(inverse.reshape(2 * NG, 2 * NG)), split_table(forward.reshape(2 * NG, 2 * NG))


def across_tables():
    y = np.arange(NG)
    j = np.arange(WIN)
    theta = angle(j, y)
    lower = np.sin(theta)
    lower[0] = np.where(y % 2 == 0, 1.0, -1.0)
    high, low = split_table(np.concatenate([np.cos(theta), lower], axis=0))
    stacked = np.concatenate([high, high, low, low], axis=0)
    wide = np.concatenate([high.T, low.T], axis=1)
    return stacked, wide


def down_tables():
    freq = np.arange(WIN) - RAD
    theta = angle(np.arange(NG), freq)
    cosine, sine = np.cos(theta) / NG**3, np.sin(theta) / NG**3
    inverse = np.block([[cosine, -sine], [sine, cosine]])
    cosine, sine = np.cos(theta).T, np.sin(theta).T
    forward = np.block([[cosine, sine], [-sine, cosine]])
    return split_table(inverse), split_table(forward)


def lane_order():
    order = np.concatenate([np.arange(WIN), [WIN], np.arange(NG - 1, WIN, -1)])
    matrix = np.zeros((NG, NG))
    matrix[order, np.arange(NG)] = 1.0
    return matrix.astype(ml_dtypes.bfloat16)


def split(value):
    high = value.astype(BF16)
    low = (value - high.astype(F32)).astype(BF16)
    return high, low


def dot(left, right, dims=((1,), (0,))):
    return lax.dot_general(left, right, (dims, ((), ())), preferred_element_type=F32)


def exponent(peak):
    return jnp.ceil(jnp.log2(jnp.maximum(peak, 1e-30)))


def encode_scale(power):
    return jnp.exp2(15.0 - power) * 0.999


def decode_scale(power):
    return jnp.exp2(power - 15.0) * (1.0 / 0.999)


def to_short(value):
    return jnp.floor(value + 0.5).astype(jnp.int32).astype(jnp.int16)


def from_short(value):
    return value.astype(jnp.int32).astype(F32)


def spread_kernel(part_ref, high_ref, low_ref, out_ref):
    powers, tails = [], []
    for band in range(BANDS):
        real = part_ref[:, 2 * band].reshape(STICKS, NG)
        imag = part_ref[:, 2 * band + 1].reshape(STICKS, NG)
        both = jnp.concatenate([real, imag], axis=1)
        field = dot(high_ref[...], both, ((1,), (1,))) + dot(low_ref[...], both, ((1,), (1,)))
        power = exponent(jnp.max(jnp.abs(field), axis=0, keepdims=True))
        field = field * encode_scale(power)
        out_ref[:, 16 * band : 16 * band + 16, :] = to_short(field[:, :NG]).reshape(RING, 16, NG)
        rest = field[:, NG:].reshape(RING, 2, 8, STICKS - NG)
        tails += [rest[:, 0], rest[:, 1]]
        powers.append(power)
    cells = part_ref[:, 2 * BANDS].reshape(STICKS, NG)
    lane = lax.broadcasted_iota(jnp.int32, (8, NG), 1)
    pick = jnp.where(lane == 0, 128.0, jnp.where(lane == 1, 1.0, 0.0))
    flat = dot(pick.astype(BF16), cells, ((1,), (1,)))[0:1]
    index = lax.broadcasted_iota(jnp.int32, (8, NG), 0)
    notes = jnp.zeros((8, NG), F32)
    for place, line in enumerate((flat, *powers)):
        tail = jnp.concatenate([line[:, NG:], jnp.zeros((1, 2 * NG - STICKS), F32)], axis=1)
        notes = jnp.where(index == 2 * place, line[:, :NG], jnp.where(index == 2 * place + 1, tail, notes))
    notes = jnp.broadcast_to(notes[None], (RING, 8, NG))
    last = jnp.concatenate([jnp.concatenate(tails, axis=2), notes], axis=1)
    out_ref[:, 32:48, :] = to_short(last)


def plane_kernel(
    me_ref, recv_ref, v0_ref, v1_ref, v2_ref, v3_ref, stack_ref, wide_ref, xa_ref, xh_ref, fh_ref, fl_ref, order_ref,
    out_ref, val_ref, low_ref, cell_ref, onehot_ref, tall_ref, flat_ref, left_a_ref, left_b_ref, mid_ref, lift_ref, tail_ref, v_ref, v_sem,
):
    copies = [
        pltpu.make_async_copy(source.at[pl.ds(0, 4 * NG), :], v_ref.at[turn], v_sem.at[turn])
        for turn, source in enumerate((v0_ref, v1_ref, v2_ref, v3_ref))
    ]
    for copy in copies:
        copy.start()

    for src in range(RING):
        val_ref[:, src * NG : (src + 1) * NG] = from_short(recv_ref[src, 0:32, :])
        last = from_short(recv_ref[src, 32:48, :])
        start = RING * NG + 32 * src
        for g in range(4):
            val_ref[8 * g : 8 * g + 8, start : start + 32] = last[:8, 32 * g : 32 * g + 32]
        for place in range(3):
            cell_ref[place : place + 1, src * NG : (src + 1) * NG] = last[8 + 2 * place : 9 + 2 * place]
            cell_ref[place : place + 1, start : start + 32] = last[9 + 2 * place : 10 + 2 * place, 0:32]

    cells = cell_ref[0:1, :].astype(jnp.int32)
    x_index = jnp.bitwise_and(lax.shift_right_logical(cells, 7) + RAD, NG - 1)
    y_index = jnp.bitwise_and(cells, NG - 1)
    onehot_ref[...] = jnp.where(
        lax.broadcasted_iota(jnp.int32, (WIN, ALL), 0) == x_index, 1.0, 0.0
    ).astype(BF16)
    pick_y = jnp.where(lax.broadcasted_iota(jnp.int32, (NG, ALL), 0) == y_index, 1.0, 0.0).astype(BF16)
    flat_ref[...] = dot(stack_ref[...], pick_y).astype(BF16)
    tall_ref[...] = dot(pick_y, wide_ref[...], ((0,), (0,))).astype(BF16)

    for band in range(BANDS):
        half = slice(16 * band, 16 * band + 16)
        value = val_ref[half, :] * decode_scale(cell_ref[1 + band : 2 + band, :])
        rounded = value.astype(BF16).astype(F32)
        low_ref[half, :] = value - rounded
        val_ref[half, :] = rounded

    lane = lax.broadcasted_iota(jnp.int32, (WIN, NG), 1)
    first = jnp.bitwise_and(lane, WIN - 1) == 0
    lower = lane < WIN

    def across(z, left_ref):
        for g in range(4):
            for part, ref in enumerate((val_ref, low_ref)):
                row = ref[pl.ds(8 * g + z, 1), :]
                spread = jnp.broadcast_to(row, (16, ALL)).astype(BF16)
                spread = jnp.concatenate([spread] * (WIN // 16), axis=0)
                at = (2 * g + part) * WIN
                left_ref[at : at + WIN, :] = spread * onehot_ref[...]
        full = dot(left_ref[...], tall_ref[...])
        full = full[:, :NG] + full[:, NG:]
        parts = [full[2 * g * WIN : (2 * g + 1) * WIN] + full[(2 * g + 1) * WIN : (2 * g + 2) * WIN] for g in range(4)]
        for band in range(BANDS):
            real, imag = parts[2 * band], parts[2 * band + 1]
            real_turn, imag_turn = pltpu.roll(real, WIN, 1), pltpu.roll(imag, WIN, 1)
            new_real = jnp.where(first, real, jnp.where(lower, real - imag_turn, real_turn + imag))
            new_imag = jnp.where(first, imag, jnp.where(lower, imag + real_turn, imag_turn - real))
            mid_ref[z, 0:WIN, band * NG : (band + 1) * NG] = new_real
            mid_ref[z, WIN:, band * NG : (band + 1) * NG] = new_imag

    @pl.loop(0, 4)
    def _(pair):
        across(2 * pair, left_a_ref)
        across(2 * pair + 1, left_b_ref)

    me = me_ref[0]
    for copy in copies:
        copy.wait()
    for turn in range(GROUP):
        for i in range(2):
            z = 2 * jnp.bitwise_xor(me, turn) + i
            at = i * NG
            potential = dot(v_ref[turn, at : at + NG, :], order_ref[...])
            potential += dot(v_ref[turn, at + 2 * NG : at + 3 * NG, :], order_ref[...])
            high, low = split(mid_ref[z])
            field = dot(xa_ref[...], jnp.concatenate([high, high], axis=0)) + dot(xh_ref[...], low)
            wide = jnp.concatenate([potential, potential], axis=1)
            weighted = field * jnp.concatenate([wide, wide], axis=0)
            high, low = split(weighted)
            folded = dot(fh_ref[...], high) + dot(fh_ref[...], low) + dot(fl_ref[...], high)
            for band in range(BANDS):
                real = folded[:WIN, band * NG : (band + 1) * NG]
                imag = folded[WIN:, band * NG : (band + 1) * NG]
                real_turn, imag_turn = pltpu.roll(real, WIN, 1), pltpu.roll(imag, WIN, 1)
                left_real = jnp.where(first, real, jnp.where(lower, real + real_turn, imag_turn - imag))
                left_imag = jnp.where(first, imag, jnp.where(lower, imag + imag_turn, real - real_turn))
                for part, value in enumerate((left_real, left_imag)):
                    high, low = split(value)
                    lift_ref[2 * band + part, z, :, 0:NG] = high
                    lift_ref[2 * band + part, z, :, NG:] = low

    @pl.loop(0, ALL // 256)
    def _(t):
        cols = pl.ds(pl.multiple_of(t * 256, 256), 256)
        select = onehot_ref[:, cols].astype(F32)[None]
        for g in range(4):
            rows = lift_ref[g].reshape(8 * WIN, 2 * NG)
            full = dot(rows, flat_ref[0:256, cols]) + dot(rows, flat_ref[256:512, cols])
            val_ref[8 * g : 8 * g + 8, cols] = jnp.sum(full.reshape(8, WIN, 256) * select, axis=1)

    for band in range(BANDS):
        half = slice(16 * band, 16 * band + 16)
        power = exponent(jnp.max(jnp.abs(val_ref[half, :]), axis=0, keepdims=True))
        cell_ref[1 + band : 2 + band, :] = power
        val_ref[half, :] = val_ref[half, :] * encode_scale(power)
    tail_ref[...] = jnp.zeros((RING, 16, NG), F32)
    for src in range(RING):
        out_ref[src, 0:32, :] = to_short(val_ref[:, src * NG : (src + 1) * NG])
        start = RING * NG + 32 * src
        for g in range(4):
            tail_ref[src, 0:8, 32 * g : 32 * g + 32] = val_ref[8 * g : 8 * g + 8, start : start + 32]
        for place in range(1, 3):
            tail_ref[src, 8 + 2 * place : 9 + 2 * place, :] = cell_ref[place : place + 1, src * NG : (src + 1) * NG]
            tail_ref[src, 9 + 2 * place : 10 + 2 * place, 0:32] = cell_ref[place : place + 1, start : start + 32]
    out_ref[:, 32:48, :] = to_short(tail_ref[...])


def finish_kernel(recv_ref, part_ref, high_ref, low_ref, out_ref, copies_ref, line_ref, pack_ref):
    squares = part_ref[:, 2 * BANDS].reshape(STICKS, NG).astype(F32)
    signed = jnp.where(squares < NG // 2, squares, squares - NG)
    across = signed * signed
    across = across[:, 0:1] + across[:, 1:2]
    k = lax.broadcasted_iota(jnp.int32, (STICKS, NG), 1)
    k = jnp.where(k < NG // 2, k, k - NG)
    total = across + (k * k).astype(F32)
    weight = jnp.where(total <= RAD * RAD, 1.0, 0.0)
    kinetic = 2.0 / (RAD * RAD) * total
    for band in range(BANDS):
        for src in range(RING):
            last = from_short(recv_ref[src, 32:48, :])
            main = from_short(recv_ref[src, 16 * band : 16 * band + 16, :])
            scale = decode_scale(last[10 + 2 * band : 12 + 2 * band])
            line_ref[16 * src : 16 * src + 16, 0:NG] = main * scale[0:1]
            for part in range(2):
                g = 2 * band + part
                at = 16 * src + 8 * part
                line_ref[at : at + 8, NG : NG + 32] = last[:8, 32 * g : 32 * g + 32] * scale[1:2, 0:32]
        high, low = split(jnp.transpose(line_ref[...])[:STICKS])
        product = dot(high, high_ref[...]) + dot(low, high_ref[...]) + dot(high, low_ref[...])
        for part in range(2):
            masked = part_ref[:, 2 * band + part].reshape(STICKS, NG).astype(F32)
            value = weight * (kinetic * masked + product[:, part * NG : (part + 1) * NG])
            value = value.reshape(GROUP, STICKS // GROUP, NG)
            out_ref[:, 2 * band + part] = value.astype(BF16)
            half = STICKS // GROUP // 2
            for src in range(GROUP):
                at = ((2 * band + part) * GROUP + src) * half
                turned = pltpu.roll(value[src, half:], NG // 2, 1)
                pack_ref[at : at + half, :] = value[src, :half] + turned
    packed = pack_ref[...].astype(BF16)
    for copy in range(copies_ref.shape[0]):
        copies_ref[copy] = packed


def vmem_call(kernel, out_shape, inputs, scratch=(), specs=None):
    vmem = pl.BlockSpec(memory_space=pltpu.VMEM)
    return pl.pallas_call(
        kernel,
        out_shape=out_shape,
        in_specs=specs or [vmem] * len(inputs),
        out_specs=jax.tree.map(lambda _: vmem, out_shape),
        scratch_shapes=list(scratch),
        compiler_params=pltpu.CompilerParams(vmem_limit_bytes=56 * 1024 * 1024),
    )(*inputs)


def spread(part):
    (high, low), _ = depth_tables()
    shape = jax.ShapeDtypeStruct((RING, ROWS, NG), jnp.int16)
    return vmem_call(spread_kernel, shape, (part, high, low))


def planes(me, recv, potentials):
    stack, wide = across_tables()
    (xh, xl), (fh, fl) = down_tables()
    xa = np.concatenate([xh, xl], axis=1)
    shape = jax.ShapeDtypeStruct((RING, ROWS, NG), jnp.int16)
    scratch = (
        pltpu.VMEM((32, ALL), F32),
        pltpu.VMEM((32, ALL), F32),
        pltpu.VMEM((8, ALL), F32),
        pltpu.VMEM((WIN, ALL), BF16),
        pltpu.VMEM((ALL, 2 * NG), BF16),
        pltpu.VMEM((4 * NG, ALL), BF16),
        pltpu.VMEM((8 * WIN, ALL), BF16),
        pltpu.VMEM((8 * WIN, ALL), BF16),
        pltpu.VMEM((8, 2 * WIN, 2 * NG), F32),
        pltpu.VMEM((4, 8, WIN, 2 * NG), BF16),
        pltpu.VMEM((RING, 16, NG), F32),
        pltpu.VMEM((GROUP, 4 * NG, NG), BF16),
        pltpu.SemaphoreType.DMA((GROUP,)),
    )
    inputs = (me, recv, *potentials, stack, wide, xa, xh, fh, fl, lane_order())
    whole = pl.BlockSpec(memory_space=pltpu.VMEM)
    specs = [pl.BlockSpec(memory_space=pltpu.SMEM), whole] + [pl.BlockSpec(memory_space=pl.ANY)] * GROUP
    specs += [whole] * (len(inputs) - 2 - GROUP)
    return vmem_call(plane_kernel, shape, inputs, scratch, specs)


def finish(recv, part, copies):
    _, (high, low) = depth_tables()
    rows = BANDS * STICKS
    shape = (
        jax.ShapeDtypeStruct((GROUP, 2 * BANDS, STICKS // GROUP, NG), BF16),
        jax.ShapeDtypeStruct((copies, rows, NG), BF16),
    )
    scratch = (pltpu.VMEM((2 * NG, 2 * NG), F32), pltpu.VMEM((rows, NG), F32))
    return vmem_call(finish_kernel, shape, (recv, part, high, low), scratch)


def pack(value):
    half = value.shape[2] // 2
    return value[:, :, :half] + jnp.roll(value[:, :, half:], NG // 2, axis=3)


def pairing(bands, vectors, axis):
    full = 0.0
    for src, left in enumerate(bands):
        right = lax.index_in_dim(vectors, src, axis, False)
        full += jnp.einsum("rkl,gbqrl->kgbq", left, right, preferred_element_type=F32)
    full = full.reshape(-1, 2, *full.shape[1:])
    real = full[:, 0, :, :, 0] + full[:, 1, :, :, 1]
    imag = full[:, 0, :, :, 1] - full[:, 1, :, :, 0]
    return jnp.stack([real, imag])


def partner(value, turn, size):
    return lax.ppermute(value, "pw", [(i, i ^ turn) for i in range(size)])


def place(pieces, me):
    for bit in (1, 2):
        odd = jnp.bitwise_and(me, bit) != 0
        pieces = [jnp.where(odd, pieces[i ^ bit], pieces[i]) for i in range(GROUP)]
    return pieces


def exchange(value, axis, groups=None):
    return lax.all_to_all(value, axis, 0, 0, axis_index_groups=groups, tiled=True)


def to_all(value, axis, count, groups=None):
    return exchange(jnp.broadcast_to(value[None], (count, *value.shape)), axis, groups)


def two_steps(value, outer, inner):
    value = value.reshape(GROUP, GROUP, *value.shape[1:])
    value = jnp.swapaxes(exchange(value, "pw", outer), 0, 1)
    return exchange(value, "pw", inner).reshape(RING, *value.shape[2:])


def per_device(block, bands, potential, stick_cells, sphere_mask):
    size = lax.axis_size("pw")
    teams = lax.axis_size("band")
    me = jnp.bitwise_and(lax.axis_index("pw"), GROUP - 1)
    own, sticks, rows = block.shape[0], block.shape[2], bands.shape[0]
    fours = [[i * GROUP + j for j in range(GROUP)] for i in range(size // GROUP)]
    far = [[i * 16 + j for i in range(GROUP)] for j in range(16)]
    near = [[k * 16 + i * GROUP + j for i in range(GROUP)] for k in range(GROUP) for j in range(GROUP)]

    inside = sphere_mask.astype(BF16)[None, None]
    masked = block * inside
    lane = jnp.arange(NG, dtype=jnp.int32)[None, :]
    column = jnp.where(lane == 0, stick_cells[:, None] // NG, jnp.where(lane == 1, stick_cells[:, None] % NG, 0))
    grouped = masked.reshape(GROUP, 2 * BANDS, sticks, NG)
    column = jnp.broadcast_to(column.astype(BF16)[None, None], (GROUP, 1, sticks, NG))
    part = exchange(jnp.concatenate([grouped, column], axis=1), "pw", fours)
    sent = spread(part)
    recv = two_steps(sent, far, near)

    bands_rows = jnp.transpose(pack(bands * inside), (2, 0, 1, 3)).reshape(-1, NG)
    v_high = lax.reduce_precision(potential, 8, 7)
    v_low = (potential - v_high).astype(BF16)
    potential_rows = jnp.stack([v_high.astype(BF16), v_low]).reshape(-1, NG)
    side = jnp.concatenate([potential_rows, bands_rows], axis=0)
    sides = [side] + [partner(side, turn, size) for turn in range(1, GROUP)]
    bands_all = place([piece[potential_rows.shape[0] :] for piece in sides], me)
    bands_all = [piece.reshape(sticks // 2, 2 * rows, NG) for piece in bands_all]
    vectors = part[:, : 2 * BANDS].reshape(GROUP * BANDS, 2, sticks, NG)
    masked_all = lax.all_gather(jnp.stack([vectors, vectors]), "band", axis=1, tiled=True)[0]
    masked_all = pack(masked_all.reshape(teams * GROUP * BANDS, 2, sticks, NG))
    masked_all = masked_all.reshape(teams, GROUP, BANDS, 2, sticks // 2, NG)

    back = two_steps(planes(me.reshape(1), recv, sides), near, far)
    result, copies = finish(back, part, teams)
    applied_all = exchange(copies, "band").reshape(teams, BANDS, 2, GROUP, sticks // 2, NG)
    pieces = [lax.dynamic_index_in_dim(result, jnp.bitwise_xor(me, turn), 0, False) for turn in range(GROUP)]
    pieces = pieces[:1] + [partner(pieces[turn], turn, size) for turn in range(1, GROUP)]
    applied = jnp.stack(place(pieces, me)).reshape(own, 2, sticks, NG)

    terms = jnp.stack([pairing(bands_all, masked_all, 1), pairing(bands_all, applied_all, 3)])
    total = jnp.sum(to_all(terms.reshape(-1, NG), "pw", GROUP, near), axis=0)
    total = jnp.sum(to_all(total, "pw", GROUP, far), axis=0)
    total = to_all(total, "pw", GROUP, fours).reshape(GROUP, 2, 2, rows, teams, BANDS)
    total = jnp.transpose(total, (1, 2, 3, 4, 0, 5)).reshape(2, 2, rows, teams * own)
    return (applied, total[0], total[1])


def solution(mesh):
    return jax.shard_map(
        per_device,
        mesh=mesh,
        in_specs=(
            P("band", None, "pw", None),
            P("band", None, "pw", None),
            P("pw", None, None),
            P("pw"),
            P("pw", None),
        ),
        out_specs=(P("band", None, "pw", None), P(None, "band", None), P(None, "band", None)),
        check_vma=False,
    )
```

```python
import jax
import jax.numpy as jnp
import ml_dtypes
import numpy as np
from jax import lax
from jax.experimental import pallas as pl
from jax.experimental.pallas import tpu as pltpu
from jax.sharding import PartitionSpec as P

NG = 128
RAD = 32
WIN = 64
GROUP = 4
RING = 16
BANDS = 2
STICKS = 160
ROWS = 48
ALL = STICKS * RING
F32 = jnp.float32
BF16 = jnp.bfloat16


def split_table(table):
    high = table.astype(ml_dtypes.bfloat16)
    low = (table - high.astype(np.float64)).astype(ml_dtypes.bfloat16)
    return high, low


def angle(first, second):
    return 2.0 * np.pi / NG * np.mod(np.outer(first, second), NG)


def depth_tables():
    k = np.arange(NG)
    theta = angle(np.arange(NG), k)
    inverse = np.zeros((RING, 2, 8, 2 * NG))
    theta = theta.reshape(RING, 8, NG)
    inverse[:, 0] = np.concatenate([np.cos(theta), -np.sin(theta)], axis=-1)
    inverse[:, 1] = np.concatenate([np.sin(theta), np.cos(theta)], axis=-1)
    forward = np.zeros((RING, 2, 8, 2 * NG))
    forward[:, 0] = np.concatenate([np.cos(theta), -np.sin(theta)], axis=-1)
    forward[:, 1] = np.concatenate([np.sin(theta), np.cos(theta)], axis=-1)
    return split_table(inverse.reshape(2 * NG, 2 * NG)), split_table(forward.reshape(2 * NG, 2 * NG))


def across_tables():
    y = np.arange(NG)
    j = np.arange(WIN)
    theta = angle(j, y)
    lower = np.sin(theta)
    lower[0] = np.where(y % 2 == 0, 1.0, -1.0)
    high, low = split_table(np.concatenate([np.cos(theta), lower], axis=0))
    stacked = np.concatenate([high, high, low, low], axis=0)
    wide = np.concatenate([high.T, low.T], axis=1)
    return stacked, wide


def down_tables():
    freq = np.arange(WIN) - RAD
    theta = angle(np.arange(NG), freq)
    cosine, sine = np.cos(theta) / NG**3, np.sin(theta) / NG**3
    inverse = np.block([[cosine, -sine], [sine, cosine]])
    cosine, sine = np.cos(theta).T, np.sin(theta).T
    forward = np.block([[cosine, sine], [-sine, cosine]])
    return split_table(inverse), split_table(forward)


def lane_order():
    order = np.concatenate([np.arange(WIN), [WIN], np.arange(NG - 1, WIN, -1)])
    matrix = np.zeros((NG, NG))
    matrix[order, np.arange(NG)] = 1.0
    return matrix.astype(ml_dtypes.bfloat16)


def split(value):
    high = value.astype(BF16)
    low = (value - high.astype(F32)).astype(BF16)
    return high, low


def dot(left, right, dims=((1,), (0,))):
    return lax.dot_general(left, right, (dims, ((), ())), preferred_element_type=F32)


def exponent(peak):
    return jnp.ceil(jnp.log2(jnp.maximum(peak, 1e-30)))


def encode_scale(power):
    return jnp.exp2(15.0 - power) * 0.999


def decode_scale(power):
    return jnp.exp2(power - 15.0) * (1.0 / 0.999)


def to_short(value):
    return jnp.floor(value + 0.5).astype(jnp.int32).astype(jnp.int16)


def from_short(value):
    return value.astype(jnp.int32).astype(F32)


def spread_kernel(part_ref, high_ref, low_ref, out_ref):
    powers, tails = [], []
    for band in range(BANDS):
        real = part_ref[:, 2 * band].reshape(STICKS, NG)
        imag = part_ref[:, 2 * band + 1].reshape(STICKS, NG)
        both = jnp.concatenate([real, imag], axis=1)
        field = dot(high_ref[...], both, ((1,), (1,))) + dot(low_ref[...], both, ((1,), (1,)))
        power = exponent(jnp.max(jnp.abs(field), axis=0, keepdims=True))
        field = field * encode_scale(power)
        out_ref[:, 16 * band : 16 * band + 16, :] = to_short(field[:, :NG]).reshape(RING, 16, NG)
        rest = field[:, NG:].reshape(RING, 2, 8, STICKS - NG)
        tails += [rest[:, 0], rest[:, 1]]
        powers.append(power)
    cells = part_ref[:, 2 * BANDS].reshape(STICKS, NG)
    lane = lax.broadcasted_iota(jnp.int32, (8, NG), 1)
    pick = jnp.where(lane == 0, 128.0, jnp.where(lane == 1, 1.0, 0.0))
    flat = dot(pick.astype(BF16), cells, ((1,), (1,)))[0:1]
    index = lax.broadcasted_iota(jnp.int32, (8, NG), 0)
    notes = jnp.zeros((8, NG), F32)
    for place, line in enumerate((flat, *powers)):
        tail = jnp.concatenate([line[:, NG:], jnp.zeros((1, 2 * NG - STICKS), F32)], axis=1)
        notes = jnp.where(index == 2 * place, line[:, :NG], jnp.where(index == 2 * place + 1, tail, notes))
    notes = jnp.broadcast_to(notes[None], (RING, 8, NG))
    last = jnp.concatenate([jnp.concatenate(tails, axis=2), notes], axis=1)
    out_ref[:, 32:48, :] = to_short(last)


def plane_kernel(
    me_ref, recv_ref, v0_ref, v1_ref, v2_ref, v3_ref, stack_ref, wide_ref, xa_ref, xh_ref, fh_ref, fl_ref, order_ref, rows_ref,
    out_ref, same_rows_ref, val_ref, low_ref, cell_ref, onehot_ref, tall_ref, flat_ref, left_a_ref, left_b_ref, mid_ref, lift_ref, tail_ref, v_ref, v_sem,
):
    copies = [
        pltpu.make_async_copy(source, v_ref.at[turn], v_sem.at[turn])
        for turn, source in enumerate((v0_ref, v1_ref, v2_ref, v3_ref))
    ]
    for copy in copies:
        copy.start()

    for src in range(RING):
        val_ref[:, src * NG : (src + 1) * NG] = from_short(recv_ref[src, 0:32, :])
        last = from_short(recv_ref[src, 32:48, :])
        start = RING * NG + 32 * src
        for g in range(4):
            val_ref[8 * g : 8 * g + 8, start : start + 32] = last[:8, 32 * g : 32 * g + 32]
        for place in range(3):
            cell_ref[place : place + 1, src * NG : (src + 1) * NG] = last[8 + 2 * place : 9 + 2 * place]
            cell_ref[place : place + 1, start : start + 32] = last[9 + 2 * place : 10 + 2 * place, 0:32]

    cells = cell_ref[0:1, :].astype(jnp.int32)
    x_index = jnp.bitwise_and(lax.shift_right_logical(cells, 7) + RAD, NG - 1)
    y_index = jnp.bitwise_and(cells, NG - 1)
    onehot_ref[...] = jnp.where(
        lax.broadcasted_iota(jnp.int32, (WIN, ALL), 0) == x_index, 1.0, 0.0
    ).astype(BF16)
    pick_y = jnp.where(lax.broadcasted_iota(jnp.int32, (NG, ALL), 0) == y_index, 1.0, 0.0).astype(BF16)
    flat_ref[...] = dot(stack_ref[...], pick_y).astype(BF16)
    tall_ref[...] = dot(pick_y, wide_ref[...], ((0,), (0,))).astype(BF16)

    for band in range(BANDS):
        half = slice(16 * band, 16 * band + 16)
        value = val_ref[half, :] * decode_scale(cell_ref[1 + band : 2 + band, :])
        rounded = value.astype(BF16).astype(F32)
        low_ref[half, :] = value - rounded
        val_ref[half, :] = rounded

    lane = lax.broadcasted_iota(jnp.int32, (WIN, NG), 1)
    first = jnp.bitwise_and(lane, WIN - 1) == 0
    lower = lane < WIN

    def across(z, left_ref):
        for g in range(4):
            for part, ref in enumerate((val_ref, low_ref)):
                row = ref[pl.ds(8 * g + z, 1), :]
                spread = jnp.broadcast_to(row, (16, ALL)).astype(BF16)
                spread = jnp.concatenate([spread] * (WIN // 16), axis=0)
                at = (2 * g + part) * WIN
                left_ref[at : at + WIN, :] = spread * onehot_ref[...]
        full = dot(left_ref[...], tall_ref[...])
        full = full[:, :NG] + full[:, NG:]
        parts = [full[2 * g * WIN : (2 * g + 1) * WIN] + full[(2 * g + 1) * WIN : (2 * g + 2) * WIN] for g in range(4)]
        for band in range(BANDS):
            real, imag = parts[2 * band], parts[2 * band + 1]
            real_turn, imag_turn = pltpu.roll(real, WIN, 1), pltpu.roll(imag, WIN, 1)
            new_real = jnp.where(first, real, jnp.where(lower, real - imag_turn, real_turn + imag))
            new_imag = jnp.where(first, imag, jnp.where(lower, imag + real_turn, imag_turn - real))
            mid_ref[z, 0:WIN, band * NG : (band + 1) * NG] = new_real
            mid_ref[z, WIN:, band * NG : (band + 1) * NG] = new_imag

    @pl.loop(0, 4)
    def _(pair):
        across(2 * pair, left_a_ref)
        across(2 * pair + 1, left_b_ref)

    me = me_ref[0]
    for copy in copies:
        copy.wait()
    for turn in range(GROUP):
        for i in range(2):
            z = 2 * jnp.bitwise_xor(me, turn) + i
            at = i * NG
            potential = dot(v_ref[turn, at : at + NG, :], order_ref[...])
            potential += dot(v_ref[turn, at + 2 * NG : at + 3 * NG, :], order_ref[...])
            high, low = split(mid_ref[z])
            field = dot(xa_ref[...], jnp.concatenate([high, high], axis=0)) + dot(xh_ref[...], low)
            wide = jnp.concatenate([potential, potential], axis=1)
            weighted = field * jnp.concatenate([wide, wide], axis=0)
            high, low = split(weighted)
            folded = dot(fh_ref[...], high) + dot(fh_ref[...], low) + dot(fl_ref[...], high)
            for band in range(BANDS):
                real = folded[:WIN, band * NG : (band + 1) * NG]
                imag = folded[WIN:, band * NG : (band + 1) * NG]
                real_turn, imag_turn = pltpu.roll(real, WIN, 1), pltpu.roll(imag, WIN, 1)
                left_real = jnp.where(first, real, jnp.where(lower, real + real_turn, imag_turn - imag))
                left_imag = jnp.where(first, imag, jnp.where(lower, imag + imag_turn, real - real_turn))
                for part, value in enumerate((left_real, left_imag)):
                    high, low = split(value)
                    lift_ref[2 * band + part, z, :, 0:NG] = high
                    lift_ref[2 * band + part, z, :, NG:] = low

    @pl.loop(0, ALL // 256)
    def _(t):
        cols = pl.ds(pl.multiple_of(t * 256, 256), 256)
        select = onehot_ref[:, cols].astype(F32)[None]
        for g in range(4):
            rows = lift_ref[g].reshape(8 * WIN, 2 * NG)
            full = dot(rows, flat_ref[0:256, cols]) + dot(rows, flat_ref[256:512, cols])
            val_ref[8 * g : 8 * g + 8, cols] = jnp.sum(full.reshape(8, WIN, 256) * select, axis=1)

    for band in range(BANDS):
        half = slice(16 * band, 16 * band + 16)
        power = exponent(jnp.max(jnp.abs(val_ref[half, :]), axis=0, keepdims=True))
        cell_ref[1 + band : 2 + band, :] = power
        val_ref[half, :] = val_ref[half, :] * encode_scale(power)
    tail_ref[...] = jnp.zeros((RING, 16, NG), F32)
    for src in range(RING):
        out_ref[src, 0:32, :] = to_short(val_ref[:, src * NG : (src + 1) * NG])
        start = RING * NG + 32 * src
        for g in range(4):
            tail_ref[src, 0:8, 32 * g : 32 * g + 32] = val_ref[8 * g : 8 * g + 8, start : start + 32]
        for place in range(1, 3):
            tail_ref[src, 8 + 2 * place : 9 + 2 * place, :] = cell_ref[place : place + 1, src * NG : (src + 1) * NG]
            tail_ref[src, 9 + 2 * place : 10 + 2 * place, 0:32] = cell_ref[place : place + 1, start : start + 32]
    out_ref[:, 32:48, :] = to_short(tail_ref[...])


def finish_kernel(recv_ref, part_ref, high_ref, low_ref, out_ref, copies_ref, line_ref, pack_ref):
    squares = part_ref[:, 2 * BANDS].reshape(STICKS, NG).astype(F32)
    signed = jnp.where(squares < NG // 2, squares, squares - NG)
    across = signed * signed
    across = across[:, 0:1] + across[:, 1:2]
    k = lax.broadcasted_iota(jnp.int32, (STICKS, NG), 1)
    k = jnp.where(k < NG // 2, k, k - NG)
    total = across + (k * k).astype(F32)
    weight = jnp.where(total <= RAD * RAD, 1.0, 0.0)
    kinetic = 2.0 / (RAD * RAD) * total
    for band in range(BANDS):
        for src in range(RING):
            last = from_short(recv_ref[src, 32:48, :])
            main = from_short(recv_ref[src, 16 * band : 16 * band + 16, :])
            scale = decode_scale(last[10 + 2 * band : 12 + 2 * band])
            line_ref[16 * src : 16 * src + 16, 0:NG] = main * scale[0:1]
            for part in range(2):
                g = 2 * band + part
                at = 16 * src + 8 * part
                line_ref[at : at + 8, NG : NG + 32] = last[:8, 32 * g : 32 * g + 32] * scale[1:2, 0:32]
        high, low = split(jnp.transpose(line_ref[...])[:STICKS])
        product = dot(high, high_ref[...]) + dot(low, high_ref[...]) + dot(high, low_ref[...])
        for part in range(2):
            masked = part_ref[:, 2 * band + part].reshape(STICKS, NG).astype(F32)
            value = weight * (kinetic * masked + product[:, part * NG : (part + 1) * NG])
            value = value.reshape(GROUP, STICKS // GROUP, NG)
            out_ref[:, 2 * band + part] = value.astype(BF16)
            half = STICKS // GROUP // 2
            for src in range(GROUP):
                at = ((2 * band + part) * GROUP + src) * half
                turned = pltpu.roll(value[src, half:], NG // 2, 1)
                pack_ref[at : at + half, :] = value[src, :half] + turned
    packed = pack_ref[...].astype(BF16)
    for copy in range(copies_ref.shape[0]):
        copies_ref[copy] = packed


def vmem_call(kernel, out_shape, inputs, scratch=(), specs=None, outs=None, aliases=None):
    vmem = pl.BlockSpec(memory_space=pltpu.VMEM)
    return pl.pallas_call(
        kernel,
        out_shape=out_shape,
        in_specs=specs or [vmem] * len(inputs),
        out_specs=outs or jax.tree.map(lambda _: vmem, out_shape),
        input_output_aliases=aliases or {},
        scratch_shapes=list(scratch),
        compiler_params=pltpu.CompilerParams(vmem_limit_bytes=56 * 1024 * 1024),
    )(*inputs)


def spread(part):
    (high, low), _ = depth_tables()
    shape = jax.ShapeDtypeStruct((RING, ROWS, NG), jnp.int16)
    return vmem_call(spread_kernel, shape, (part, high, low))


def planes(me, recv, potentials, rows):
    stack, wide = across_tables()
    (xh, xl), (fh, fl) = down_tables()
    xa = np.concatenate([xh, xl], axis=1)
    shape = (jax.ShapeDtypeStruct((RING, ROWS, NG), jnp.int16), jax.ShapeDtypeStruct(rows.shape, rows.dtype))
    scratch = (
        pltpu.VMEM((32, ALL), F32),
        pltpu.VMEM((32, ALL), F32),
        pltpu.VMEM((8, ALL), F32),
        pltpu.VMEM((WIN, ALL), BF16),
        pltpu.VMEM((ALL, 2 * NG), BF16),
        pltpu.VMEM((4 * NG, ALL), BF16),
        pltpu.VMEM((8 * WIN, ALL), BF16),
        pltpu.VMEM((8 * WIN, ALL), BF16),
        pltpu.VMEM((8, 2 * WIN, 2 * NG), F32),
        pltpu.VMEM((4, 8, WIN, 2 * NG), BF16),
        pltpu.VMEM((RING, 16, NG), F32),
        pltpu.VMEM((GROUP, 4 * NG, NG), BF16),
        pltpu.SemaphoreType.DMA((GROUP,)),
    )
    inputs = (me, recv, *potentials, stack, wide, xa, xh, fh, fl, lane_order(), rows)
    whole = pl.BlockSpec(memory_space=pltpu.VMEM)
    specs = [pl.BlockSpec(memory_space=pltpu.SMEM), whole] + [pl.BlockSpec(memory_space=pl.ANY)] * GROUP
    specs += [whole] * (len(inputs) - 3 - GROUP) + [pl.BlockSpec(memory_space=pl.ANY)]
    outs = (whole, pl.BlockSpec(memory_space=pl.ANY))
    return vmem_call(plane_kernel, shape, inputs, scratch, specs, outs, {len(inputs) - 1: 1})


def finish(recv, part, copies):
    _, (high, low) = depth_tables()
    rows = BANDS * STICKS
    shape = (
        jax.ShapeDtypeStruct((GROUP, 2 * BANDS, STICKS // GROUP, NG), BF16),
        jax.ShapeDtypeStruct((copies, rows, NG), BF16),
    )
    scratch = (pltpu.VMEM((2 * NG, 2 * NG), F32), pltpu.VMEM((rows, NG), F32))
    return vmem_call(finish_kernel, shape, (recv, part, high, low), scratch)


def pack(value):
    half = value.shape[2] // 2
    return value[:, :, :half] + jnp.roll(value[:, :, half:], NG // 2, axis=3)


def pairing(bands, vectors, axis):
    full = 0.0
    for src, left in enumerate(bands):
        right = lax.index_in_dim(vectors, src, axis, False)
        full += jnp.einsum("rkl,gbqrl->kgbq", left, right, preferred_element_type=F32)
    full = full.reshape(-1, 2, *full.shape[1:])
    real = full[:, 0, :, :, 0] + full[:, 1, :, :, 1]
    imag = full[:, 0, :, :, 1] - full[:, 1, :, :, 0]
    return jnp.stack([real, imag])


def partner(value, turn, size):
    return lax.ppermute(value, "pw", [(i, i ^ turn) for i in range(size)])


def place(pieces, me):
    for bit in (1, 2):
        odd = jnp.bitwise_and(me, bit) != 0
        pieces = [jnp.where(odd, pieces[i ^ bit], pieces[i]) for i in range(GROUP)]
    return pieces


def exchange(value, axis, groups=None):
    return lax.all_to_all(value, axis, 0, 0, axis_index_groups=groups, tiled=True)


def to_all(value, axis, count, groups=None):
    return exchange(jnp.broadcast_to(value[None], (count, *value.shape)), axis, groups)


def per_device(block, bands, potential, stick_cells, sphere_mask):
    size = lax.axis_size("pw")
    teams = lax.axis_size("band")
    me = jnp.bitwise_and(lax.axis_index("pw"), GROUP - 1)
    own, sticks, rows = block.shape[0], block.shape[2], bands.shape[0]
    fours = [[i * GROUP + j for j in range(GROUP)] for i in range(size // GROUP)]
    rings = [[i * GROUP + j for i in range(size // GROUP)] for j in range(GROUP)]

    inside = sphere_mask.astype(BF16)[None, None]
    masked = block * inside
    lane = jnp.arange(NG, dtype=jnp.int32)[None, :]
    column = jnp.where(lane == 0, stick_cells[:, None] // NG, jnp.where(lane == 1, stick_cells[:, None] % NG, 0))
    grouped = masked.reshape(GROUP, 2 * BANDS, sticks, NG)
    column = jnp.broadcast_to(column.astype(BF16)[None, None], (GROUP, 1, sticks, NG))
    part = exchange(jnp.concatenate([grouped, column], axis=1), "pw", fours)
    sent = spread(part)
    recv = exchange(sent, "pw", rings)

    bands_rows = jnp.transpose(pack(bands * inside), (2, 0, 1, 3)).reshape(-1, NG)
    v_high = lax.reduce_precision(potential, 8, 7)
    v_low = (potential - v_high).astype(BF16)
    potential_rows = jnp.stack([v_high.astype(BF16), v_low]).reshape(-1, NG)
    potentials = [potential_rows] + [partner(potential_rows, turn, size) for turn in range(1, GROUP)]
    back, bands_rows = planes(me.reshape(1), recv, potentials, bands_rows)
    back = exchange(back, "pw", rings)
    bands_all = place([bands_rows] + [partner(bands_rows, turn, size) for turn in range(1, GROUP)], me)
    bands_all = [piece.reshape(sticks // 2, 2 * rows, NG) for piece in bands_all]
    vectors = part[:, : 2 * BANDS].reshape(GROUP * BANDS, 2, sticks, NG)
    masked_all = lax.all_gather(jnp.stack([vectors, vectors]), "band", axis=1, tiled=True)[0]
    masked_all = pack(masked_all.reshape(teams * GROUP * BANDS, 2, sticks, NG))
    masked_all = masked_all.reshape(teams, GROUP, BANDS, 2, sticks // 2, NG)

    result, copies = finish(back, part, teams)
    applied_all = exchange(copies, "band").reshape(teams, BANDS, 2, GROUP, sticks // 2, NG)
    pieces = [lax.dynamic_index_in_dim(result, jnp.bitwise_xor(me, turn), 0, False) for turn in range(GROUP)]
    pieces = pieces[:1] + [partner(pieces[turn], turn, size) for turn in range(1, GROUP)]
    applied = jnp.stack(place(pieces, me)).reshape(own, 2, sticks, NG)

    terms = jnp.stack([pairing(bands_all, masked_all, 1), pairing(bands_all, applied_all, 3)])
    total = jnp.sum(to_all(terms.reshape(-1, NG), "pw", size // GROUP, rings), axis=0)
    total = to_all(total, "pw", GROUP, fours).reshape(GROUP, 2, 2, rows, teams, BANDS)
    total = jnp.transpose(total, (1, 2, 3, 4, 0, 5)).reshape(2, 2, rows, teams * own)
    return (applied, total[0], total[1])


def solution(mesh):
    return jax.shard_map(
        per_device,
        mesh=mesh,
        in_specs=(
            P("band", None, "pw", None),
            P("band", None, "pw", None),
            P("pw", None, None),
            P("pw"),
            P("pw", None),
        ),
        out_specs=(P("band", None, "pw", None), P(None, "band", None), P(None, "band", None)),
        check_vma=False,
    )
```

```python
import jax
import jax.numpy as jnp
import ml_dtypes
import numpy as np
from jax import lax
from jax.experimental import pallas as pl
from jax.experimental.pallas import tpu as pltpu
from jax.sharding import PartitionSpec as P

NG = 128
RAD = 32
WIN = 64
GROUP = 4
RING = 16
BANDS = 2
STICKS = 160
ROWS = 48
ALL = STICKS * RING
F32 = jnp.float32
BF16 = jnp.bfloat16


def split_table(table):
    high = table.astype(ml_dtypes.bfloat16)
    low = (table - high.astype(np.float64)).astype(ml_dtypes.bfloat16)
    return high, low


def angle(first, second):
    return 2.0 * np.pi / NG * np.mod(np.outer(first, second), NG)


def depth_tables():
    k = np.arange(NG)
    theta = angle(np.arange(NG), k)
    inverse = np.zeros((RING, 2, 8, 2 * NG))
    theta = theta.reshape(RING, 8, NG)
    inverse[:, 0] = np.concatenate([np.cos(theta), -np.sin(theta)], axis=-1)
    inverse[:, 1] = np.concatenate([np.sin(theta), np.cos(theta)], axis=-1)
    forward = np.zeros((RING, 2, 8, 2 * NG))
    forward[:, 0] = np.concatenate([np.cos(theta), -np.sin(theta)], axis=-1)
    forward[:, 1] = np.concatenate([np.sin(theta), np.cos(theta)], axis=-1)
    return split_table(inverse.reshape(2 * NG, 2 * NG)), split_table(forward.reshape(2 * NG, 2 * NG))


def across_tables():
    y = np.arange(NG)
    j = np.arange(WIN)
    theta = angle(j, y)
    lower = np.sin(theta)
    lower[0] = np.where(y % 2 == 0, 1.0, -1.0)
    high, low = split_table(np.concatenate([np.cos(theta), lower], axis=0))
    stacked = np.concatenate([high, high, low, low], axis=0)
    wide = np.concatenate([high.T, low.T], axis=1)
    return stacked, wide


def down_tables():
    freq = np.arange(WIN) - RAD
    theta = angle(np.arange(NG), freq)
    cosine, sine = np.cos(theta) / NG**3, np.sin(theta) / NG**3
    inverse = np.block([[cosine, -sine], [sine, cosine]])
    cosine, sine = np.cos(theta).T, np.sin(theta).T
    forward = np.block([[cosine, sine], [-sine, cosine]])
    return split_table(inverse), split_table(forward)


def lane_order():
    order = np.concatenate([np.arange(WIN), [WIN], np.arange(NG - 1, WIN, -1)])
    matrix = np.zeros((NG, NG))
    matrix[order, np.arange(NG)] = 1.0
    return matrix.astype(ml_dtypes.bfloat16)


def split(value):
    high = value.astype(BF16)
    low = (value - high.astype(F32)).astype(BF16)
    return high, low


def dot(left, right, dims=((1,), (0,))):
    return lax.dot_general(left, right, (dims, ((), ())), preferred_element_type=F32)


def exponent(peak):
    return jnp.ceil(jnp.log2(jnp.maximum(peak, 1e-30)))


def encode_scale(power):
    return jnp.exp2(15.0 - power) * 0.999


def decode_scale(power):
    return jnp.exp2(power - 15.0) * (1.0 / 0.999)


def to_short(value):
    return jnp.floor(value + 0.5).astype(jnp.int32).astype(jnp.int16)


def from_short(value):
    return value.astype(jnp.int32).astype(F32)


def group_kernel(cells_ref, block_ref, mask_ref, out_ref, column_ref):
    sticks = mask_ref.shape[0]
    inside = jnp.where(mask_ref[...] > 0, 1.0, 0.0)
    lane = lax.broadcasted_iota(jnp.int32, (1, NG), 1)
    for s in range(sticks):
        cell = cells_ref[s]
        x, y = lax.shift_right_logical(cell, 7), jnp.bitwise_and(cell, NG - 1)
        column_ref[s : s + 1, :] = jnp.where(lane == 0, x, jnp.where(lane == 1, y, 0)).astype(F32)
    column = column_ref[...].astype(BF16)
    for group in range(GROUP):
        for line in range(2 * BANDS):
            value = block_ref[BANDS * group + line // 2, line % 2].astype(F32) * inside
            out_ref[group, line] = value.astype(BF16)
        out_ref[group, 2 * BANDS] = column


def spread_kernel(part_ref, high_ref, low_ref, rows_ref, out_ref, vectors_ref, same_rows_ref):
    for src in range(GROUP):
        for band in range(BANDS):
            for copy in range(vectors_ref.shape[0]):
                vectors_ref[copy, BANDS * src + band] = part_ref[src, 2 * band : 2 * band + 2]
    powers, tails = [], []
    for band in range(BANDS):
        real = part_ref[:, 2 * band].reshape(STICKS, NG)
        imag = part_ref[:, 2 * band + 1].reshape(STICKS, NG)
        both = jnp.concatenate([real, imag], axis=1)
        field = dot(high_ref[...], both, ((1,), (1,))) + dot(low_ref[...], both, ((1,), (1,)))
        power = exponent(jnp.max(jnp.abs(field), axis=0, keepdims=True))
        field = field * encode_scale(power)
        out_ref[:, 16 * band : 16 * band + 16, :] = to_short(field[:, :NG]).reshape(RING, 16, NG)
        rest = field[:, NG:].reshape(RING, 2, 8, STICKS - NG)
        tails += [rest[:, 0], rest[:, 1]]
        powers.append(power)
    cells = part_ref[:, 2 * BANDS].reshape(STICKS, NG)
    lane = lax.broadcasted_iota(jnp.int32, (8, NG), 1)
    pick = jnp.where(lane == 0, 128.0, jnp.where(lane == 1, 1.0, 0.0))
    flat = dot(pick.astype(BF16), cells, ((1,), (1,)))[0:1]
    index = lax.broadcasted_iota(jnp.int32, (8, NG), 0)
    notes = jnp.zeros((8, NG), F32)
    for place, line in enumerate((flat, *powers)):
        tail = jnp.concatenate([line[:, NG:], jnp.zeros((1, 2 * NG - STICKS), F32)], axis=1)
        notes = jnp.where(index == 2 * place, line[:, :NG], jnp.where(index == 2 * place + 1, tail, notes))
    notes = jnp.broadcast_to(notes[None], (RING, 8, NG))
    last = jnp.concatenate([jnp.concatenate(tails, axis=2), notes], axis=1)
    out_ref[:, 32:48, :] = to_short(last)


def plane_kernel(
    me_ref, recv_ref, v0_ref, v1_ref, v2_ref, v3_ref, stack_ref, wide_ref, xa_ref, xh_ref, fh_ref, fl_ref, order_ref, rows_ref,
    out_ref, same_rows_ref, val_ref, low_ref, cell_ref, onehot_ref, tall_ref, flat_ref, left_a_ref, left_b_ref, mid_ref, lift_ref, tail_ref, v_ref, v_sem,
):
    copies = [
        pltpu.make_async_copy(source, v_ref.at[turn], v_sem.at[turn])
        for turn, source in enumerate((v0_ref, v1_ref, v2_ref, v3_ref))
    ]
    for copy in copies:
        copy.start()

    for src in range(RING):
        val_ref[:, src * NG : (src + 1) * NG] = from_short(recv_ref[src, 0:32, :])
        last = from_short(recv_ref[src, 32:48, :])
        start = RING * NG + 32 * src
        for g in range(4):
            val_ref[8 * g : 8 * g + 8, start : start + 32] = last[:8, 32 * g : 32 * g + 32]
        for place in range(3):
            cell_ref[place : place + 1, src * NG : (src + 1) * NG] = last[8 + 2 * place : 9 + 2 * place]
            cell_ref[place : place + 1, start : start + 32] = last[9 + 2 * place : 10 + 2 * place, 0:32]

    cells = cell_ref[0:1, :].astype(jnp.int32)
    x_index = jnp.bitwise_and(lax.shift_right_logical(cells, 7) + RAD, NG - 1)
    y_index = jnp.bitwise_and(cells, NG - 1)
    onehot_ref[...] = jnp.where(
        lax.broadcasted_iota(jnp.int32, (WIN, ALL), 0) == x_index, 1.0, 0.0
    ).astype(BF16)
    pick_y = jnp.where(lax.broadcasted_iota(jnp.int32, (NG, ALL), 0) == y_index, 1.0, 0.0).astype(BF16)
    flat_ref[...] = dot(stack_ref[...], pick_y).astype(BF16)
    tall_ref[...] = dot(pick_y, wide_ref[...], ((0,), (0,))).astype(BF16)

    for band in range(BANDS):
        half = slice(16 * band, 16 * band + 16)
        value = val_ref[half, :] * decode_scale(cell_ref[1 + band : 2 + band, :])
        rounded = value.astype(BF16).astype(F32)
        low_ref[half, :] = value - rounded
        val_ref[half, :] = rounded

    lane = lax.broadcasted_iota(jnp.int32, (WIN, NG), 1)
    first = jnp.bitwise_and(lane, WIN - 1) == 0
    lower = lane < WIN

    def across(z, left_ref):
        for g in range(4):
            for part, ref in enumerate((val_ref, low_ref)):
                row = ref[pl.ds(8 * g + z, 1), :]
                spread = jnp.broadcast_to(row, (16, ALL)).astype(BF16)
                spread = jnp.concatenate([spread] * (WIN // 16), axis=0)
                at = (2 * g + part) * WIN
                left_ref[at : at + WIN, :] = spread * onehot_ref[...]
        full = dot(left_ref[...], tall_ref[...])
        full = full[:, :NG] + full[:, NG:]
        parts = [full[2 * g * WIN : (2 * g + 1) * WIN] + full[(2 * g + 1) * WIN : (2 * g + 2) * WIN] for g in range(4)]
        for band in range(BANDS):
            real, imag = parts[2 * band], parts[2 * band + 1]
            real_turn, imag_turn = pltpu.roll(real, WIN, 1), pltpu.roll(imag, WIN, 1)
            new_real = jnp.where(first, real, jnp.where(lower, real - imag_turn, real_turn + imag))
            new_imag = jnp.where(first, imag, jnp.where(lower, imag + real_turn, imag_turn - real))
            mid_ref[z, 0:WIN, band * NG : (band + 1) * NG] = new_real
            mid_ref[z, WIN:, band * NG : (band + 1) * NG] = new_imag

    @pl.loop(0, 4)
    def _(pair):
        across(2 * pair, left_a_ref)
        across(2 * pair + 1, left_b_ref)

    me = me_ref[0]
    for copy in copies:
        copy.wait()
    for turn in range(GROUP):
        for i in range(2):
            z = 2 * jnp.bitwise_xor(me, turn) + i
            at = i * NG
            potential = dot(v_ref[turn, at : at + NG, :], order_ref[...])
            potential += dot(v_ref[turn, at + 2 * NG : at + 3 * NG, :], order_ref[...])
            high, low = split(mid_ref[z])
            field = dot(xa_ref[...], jnp.concatenate([high, high], axis=0)) + dot(xh_ref[...], low)
            wide = jnp.concatenate([potential, potential], axis=1)
            weighted = field * jnp.concatenate([wide, wide], axis=0)
            high, low = split(weighted)
            folded = dot(fh_ref[...], high) + dot(fh_ref[...], low) + dot(fl_ref[...], high)
            for band in range(BANDS):
                real = folded[:WIN, band * NG : (band + 1) * NG]
                imag = folded[WIN:, band * NG : (band + 1) * NG]
                real_turn, imag_turn = pltpu.roll(real, WIN, 1), pltpu.roll(imag, WIN, 1)
                left_real = jnp.where(first, real, jnp.where(lower, real + real_turn, imag_turn - imag))
                left_imag = jnp.where(first, imag, jnp.where(lower, imag + imag_turn, real - real_turn))
                for part, value in enumerate((left_real, left_imag)):
                    high, low = split(value)
                    lift_ref[2 * band + part, z, :, 0:NG] = high
                    lift_ref[2 * band + part, z, :, NG:] = low

    @pl.loop(0, ALL // 256)
    def _(t):
        cols = pl.ds(pl.multiple_of(t * 256, 256), 256)
        select = onehot_ref[:, cols].astype(F32)[None]
        for g in range(4):
            rows = lift_ref[g].reshape(8 * WIN, 2 * NG)
            full = dot(rows, flat_ref[0:256, cols]) + dot(rows, flat_ref[256:512, cols])
            val_ref[8 * g : 8 * g + 8, cols] = jnp.sum(full.reshape(8, WIN, 256) * select, axis=1)

    for band in range(BANDS):
        half = slice(16 * band, 16 * band + 16)
        power = exponent(jnp.max(jnp.abs(val_ref[half, :]), axis=0, keepdims=True))
        cell_ref[1 + band : 2 + band, :] = power
        val_ref[half, :] = val_ref[half, :] * encode_scale(power)
    tail_ref[...] = jnp.zeros((RING, 16, NG), F32)
    for src in range(RING):
        out_ref[src, 0:32, :] = to_short(val_ref[:, src * NG : (src + 1) * NG])
        start = RING * NG + 32 * src
        for g in range(4):
            tail_ref[src, 0:8, 32 * g : 32 * g + 32] = val_ref[8 * g : 8 * g + 8, start : start + 32]
        for place in range(1, 3):
            tail_ref[src, 8 + 2 * place : 9 + 2 * place, :] = cell_ref[place : place + 1, src * NG : (src + 1) * NG]
            tail_ref[src, 9 + 2 * place : 10 + 2 * place, 0:32] = cell_ref[place : place + 1, start : start + 32]
    out_ref[:, 32:48, :] = to_short(tail_ref[...])


def finish_kernel(
    recv_ref, part_ref, high_ref, low_ref, rows_ref, out_ref, copies_ref, same_rows_ref, line_ref, pack_ref
):
    squares = part_ref[:, 2 * BANDS].reshape(STICKS, NG).astype(F32)
    signed = jnp.where(squares < NG // 2, squares, squares - NG)
    across = signed * signed
    across = across[:, 0:1] + across[:, 1:2]
    k = lax.broadcasted_iota(jnp.int32, (STICKS, NG), 1)
    k = jnp.where(k < NG // 2, k, k - NG)
    total = across + (k * k).astype(F32)
    weight = jnp.where(total <= RAD * RAD, 1.0, 0.0)
    kinetic = 2.0 / (RAD * RAD) * total
    for band in range(BANDS):
        for src in range(RING):
            last = from_short(recv_ref[src, 32:48, :])
            main = from_short(recv_ref[src, 16 * band : 16 * band + 16, :])
            scale = decode_scale(last[10 + 2 * band : 12 + 2 * band])
            line_ref[16 * src : 16 * src + 16, 0:NG] = main * scale[0:1]
            for part in range(2):
                g = 2 * band + part
                at = 16 * src + 8 * part
                line_ref[at : at + 8, NG : NG + 32] = last[:8, 32 * g : 32 * g + 32] * scale[1:2, 0:32]
        high, low = split(jnp.transpose(line_ref[...])[:STICKS])
        product = dot(high, high_ref[...]) + dot(low, high_ref[...]) + dot(high, low_ref[...])
        for part in range(2):
            masked = part_ref[:, 2 * band + part].reshape(STICKS, NG).astype(F32)
            value = weight * (kinetic * masked + product[:, part * NG : (part + 1) * NG])
            value = value.reshape(GROUP, STICKS // GROUP, NG)
            out_ref[:, 2 * band + part] = value.astype(BF16)
            half = STICKS // GROUP // 2
            for src in range(GROUP):
                at = ((2 * band + part) * GROUP + src) * half
                turned = pltpu.roll(value[src, half:], NG // 2, 1)
                pack_ref[at : at + half, :] = value[src, :half] + turned
    packed = pack_ref[...].astype(BF16)
    for copy in range(copies_ref.shape[0]):
        copies_ref[copy] = packed


def vmem_call(kernel, out_shape, inputs, scratch=(), specs=None, outs=None, aliases=None):
    vmem = pl.BlockSpec(memory_space=pltpu.VMEM)
    return pl.pallas_call(
        kernel,
        out_shape=out_shape,
        in_specs=specs or [vmem] * len(inputs),
        out_specs=outs or jax.tree.map(lambda _: vmem, out_shape),
        input_output_aliases=aliases or {},
        scratch_shapes=list(scratch),
        compiler_params=pltpu.CompilerParams(vmem_limit_bytes=56 * 1024 * 1024),
    )(*inputs)


def group(stick_cells, block, sphere_mask):
    sticks = block.shape[2]
    shape = jax.ShapeDtypeStruct((GROUP, 2 * BANDS + 1, sticks, NG), BF16)
    whole = pl.BlockSpec(memory_space=pltpu.VMEM)
    specs = [pl.BlockSpec(memory_space=pltpu.SMEM), whole, whole]
    inputs = (stick_cells, block, sphere_mask)
    return vmem_call(group_kernel, shape, inputs, (pltpu.VMEM((sticks, NG), F32),), specs)


def spread(part, rows):
    (high, low), _ = depth_tables()
    shape = (
        jax.ShapeDtypeStruct((RING, ROWS, NG), jnp.int16),
        jax.ShapeDtypeStruct((2, GROUP * BANDS, 2, *part.shape[2:]), BF16),
        jax.ShapeDtypeStruct(rows.shape, rows.dtype),
    )
    whole, place = pl.BlockSpec(memory_space=pltpu.VMEM), pl.BlockSpec(memory_space=pl.ANY)
    inputs = (part, high, low, rows)
    return vmem_call(spread_kernel, shape, inputs, (), [whole] * 3 + [place], (whole, whole, place), {3: 2})


def planes(me, recv, potentials, rows):
    stack, wide = across_tables()
    (xh, xl), (fh, fl) = down_tables()
    xa = np.concatenate([xh, xl], axis=1)
    shape = (jax.ShapeDtypeStruct((RING, ROWS, NG), jnp.int16), jax.ShapeDtypeStruct(rows.shape, rows.dtype))
    scratch = (
        pltpu.VMEM((32, ALL), F32),
        pltpu.VMEM((32, ALL), F32),
        pltpu.VMEM((8, ALL), F32),
        pltpu.VMEM((WIN, ALL), BF16),
        pltpu.VMEM((ALL, 2 * NG), BF16),
        pltpu.VMEM((4 * NG, ALL), BF16),
        pltpu.VMEM((8 * WIN, ALL), BF16),
        pltpu.VMEM((8 * WIN, ALL), BF16),
        pltpu.VMEM((8, 2 * WIN, 2 * NG), F32),
        pltpu.VMEM((4, 8, WIN, 2 * NG), BF16),
        pltpu.VMEM((RING, 16, NG), F32),
        pltpu.VMEM((GROUP, 4 * NG, NG), BF16),
        pltpu.SemaphoreType.DMA((GROUP,)),
    )
    inputs = (me, recv, *potentials, stack, wide, xa, xh, fh, fl, lane_order(), rows)
    whole = pl.BlockSpec(memory_space=pltpu.VMEM)
    specs = [pl.BlockSpec(memory_space=pltpu.SMEM), whole] + [pl.BlockSpec(memory_space=pl.ANY)] * GROUP
    specs += [whole] * (len(inputs) - 3 - GROUP) + [pl.BlockSpec(memory_space=pl.ANY)]
    outs = (whole, pl.BlockSpec(memory_space=pl.ANY))
    return vmem_call(plane_kernel, shape, inputs, scratch, specs, outs, {len(inputs) - 1: 1})


def finish(recv, part, copies, other):
    _, (high, low) = depth_tables()
    rows = BANDS * STICKS
    shape = (
        jax.ShapeDtypeStruct((GROUP, 2 * BANDS, STICKS // GROUP, NG), BF16),
        jax.ShapeDtypeStruct((copies, rows, NG), BF16),
        jax.ShapeDtypeStruct(other.shape, other.dtype),
    )
    scratch = (pltpu.VMEM((2 * NG, 2 * NG), F32), pltpu.VMEM((rows, NG), F32))
    whole, place = pl.BlockSpec(memory_space=pltpu.VMEM), pl.BlockSpec(memory_space=pl.ANY)
    inputs = (recv, part, high, low, other)
    return vmem_call(finish_kernel, shape, inputs, scratch, [whole] * 4 + [place], (whole, whole, place), {4: 2})


def pack(value):
    half = value.shape[2] // 2
    return value[:, :, :half] + jnp.roll(value[:, :, half:], NG // 2, axis=3)


def pairing(bands, vectors, axis):
    full = 0.0
    for src, left in enumerate(bands):
        right = lax.index_in_dim(vectors, src, axis, False)
        full += jnp.einsum("rkl,gbqrl->kgbq", left, right, preferred_element_type=F32)
    full = full.reshape(-1, 2, *full.shape[1:])
    real = full[:, 0, :, :, 0] + full[:, 1, :, :, 1]
    imag = full[:, 0, :, :, 1] - full[:, 1, :, :, 0]
    return jnp.stack([real, imag])


def partner(value, turn, size):
    return lax.ppermute(value, "pw", [(i, i ^ turn) for i in range(size)])


def place(pieces, me):
    for bit in (1, 2):
        odd = jnp.bitwise_and(me, bit) != 0
        pieces = [jnp.where(odd, pieces[i ^ bit], pieces[i]) for i in range(GROUP)]
    return pieces


def exchange(value, axis, groups=None):
    return lax.all_to_all(value, axis, 0, 0, axis_index_groups=groups, tiled=True)


def to_all(value, axis, count, groups=None):
    return exchange(jnp.broadcast_to(value[None], (count, *value.shape)), axis, groups)


def per_device(block, bands, potential, stick_cells, sphere_mask):
    size = lax.axis_size("pw")
    teams = lax.axis_size("band")
    me = jnp.bitwise_and(lax.axis_index("pw"), GROUP - 1)
    own, sticks, rows = block.shape[0], block.shape[2], bands.shape[0]
    fours = [[i * GROUP + j for j in range(GROUP)] for i in range(size // GROUP)]
    rings = [[i * GROUP + j for i in range(size // GROUP)] for j in range(GROUP)]

    part = exchange(group(stick_cells, block, sphere_mask), "pw", fours)
    v_high = lax.reduce_precision(potential, 8, 7)
    v_low = (potential - v_high).astype(BF16)
    potential_rows = jnp.stack([v_high.astype(BF16), v_low]).reshape(-1, NG)
    sent, vectors, potential_rows = spread(part, potential_rows)
    recv = exchange(sent, "pw", rings)

    inside = sphere_mask.astype(BF16)[None, None]
    bands_rows = jnp.transpose(pack(bands * inside), (2, 0, 1, 3)).reshape(-1, NG)
    potentials = [potential_rows] + [partner(potential_rows, turn, size) for turn in range(1, GROUP)]
    back, bands_rows = planes(me.reshape(1), recv, potentials, bands_rows)
    back = exchange(back, "pw", rings)
    bands_all = place([bands_rows] + [partner(bands_rows, turn, size) for turn in range(1, GROUP)], me)
    bands_all = [piece.reshape(sticks // 2, 2 * rows, NG) for piece in bands_all]
    masked_all = lax.all_gather(vectors, "band", axis=1, tiled=True)[0]
    masked_all = pack(masked_all.reshape(teams * GROUP * BANDS, 2, sticks, NG))
    masked_all = masked_all.reshape(teams, GROUP, BANDS, 2, sticks // 2, NG)

    result, copies, masked_all = finish(back, part, teams, masked_all)
    applied_all = exchange(copies, "band").reshape(teams, BANDS, 2, GROUP, sticks // 2, NG)
    pieces = [lax.dynamic_index_in_dim(result, jnp.bitwise_xor(me, turn), 0, False) for turn in range(GROUP)]
    pieces = pieces[:1] + [partner(pieces[turn], turn, size) for turn in range(1, GROUP)]
    applied = jnp.stack(place(pieces, me)).reshape(own, 2, sticks, NG)

    terms = jnp.stack([pairing(bands_all, masked_all, 1), pairing(bands_all, applied_all, 3)])
    total = jnp.sum(to_all(terms.reshape(-1, NG), "pw", size // GROUP, rings), axis=0)
    total = to_all(total, "pw", GROUP, fours).reshape(GROUP, 2, 2, rows, teams, BANDS)
    total = jnp.transpose(total, (1, 2, 3, 4, 0, 5)).reshape(2, 2, rows, teams * own)
    return (applied, total[0], total[1])


def solution(mesh):
    return jax.shard_map(
        per_device,
        mesh=mesh,
        in_specs=(
            P("band", None, "pw", None),
            P("band", None, "pw", None),
            P("pw", None, None),
            P("pw"),
            P("pw", None),
        ),
        out_specs=(P("band", None, "pw", None), P(None, "band", None), P(None, "band", None)),
        check_vma=False,
    )
```

```python
import jax
import jax.numpy as jnp
import ml_dtypes
import numpy as np
from jax import lax
from jax.experimental import pallas as pl
from jax.experimental.pallas import tpu as pltpu
from jax.sharding import PartitionSpec as P

NG = 128
RAD = 32
WIN = 64
GROUP = 4
RING = 16
BANDS = 2
STICKS = 160
ROWS = 48
ALL = STICKS * RING
F32 = jnp.float32
BF16 = jnp.bfloat16


def split_table(table):
    high = table.astype(ml_dtypes.bfloat16)
    low = (table - high.astype(np.float64)).astype(ml_dtypes.bfloat16)
    return high, low


def angle(first, second):
    return 2.0 * np.pi / NG * np.mod(np.outer(first, second), NG)


def depth_tables():
    k = np.arange(NG)
    theta = angle(np.arange(NG), k)
    inverse = np.zeros((RING, 2, 8, 2 * NG))
    theta = theta.reshape(RING, 8, NG)
    inverse[:, 0] = np.concatenate([np.cos(theta), -np.sin(theta)], axis=-1)
    inverse[:, 1] = np.concatenate([np.sin(theta), np.cos(theta)], axis=-1)
    forward = np.zeros((RING, 2, 8, 2 * NG))
    forward[:, 0] = np.concatenate([np.cos(theta), -np.sin(theta)], axis=-1)
    forward[:, 1] = np.concatenate([np.sin(theta), np.cos(theta)], axis=-1)
    return split_table(inverse.reshape(2 * NG, 2 * NG)), split_table(forward.reshape(2 * NG, 2 * NG))


def across_tables():
    y = np.arange(NG)
    j = np.arange(WIN)
    theta = angle(j, y)
    lower = np.sin(theta)
    lower[0] = np.where(y % 2 == 0, 1.0, -1.0)
    high, low = split_table(np.concatenate([np.cos(theta), lower], axis=0))
    stacked = np.concatenate([high, high, low, low], axis=0)
    wide = np.concatenate([high.T, low.T], axis=1)
    return stacked, wide


def down_tables():
    freq = np.arange(WIN) - RAD
    theta = angle(np.arange(NG), freq)
    cosine, sine = np.cos(theta) / NG**3, np.sin(theta) / NG**3
    inverse = np.block([[cosine, -sine], [sine, cosine]])
    cosine, sine = np.cos(theta).T, np.sin(theta).T
    forward = np.block([[cosine, sine], [-sine, cosine]])
    return split_table(inverse), split_table(forward)


def lane_order():
    order = np.concatenate([np.arange(WIN), [WIN], np.arange(NG - 1, WIN, -1)])
    matrix = np.zeros((NG, NG))
    matrix[order, np.arange(NG)] = 1.0
    return matrix.astype(ml_dtypes.bfloat16)


def split(value):
    high = value.astype(BF16)
    low = (value - high.astype(F32)).astype(BF16)
    return high, low


def dot(left, right, dims=((1,), (0,))):
    return lax.dot_general(left, right, (dims, ((), ())), preferred_element_type=F32)


def exponent(peak):
    return jnp.ceil(jnp.log2(jnp.maximum(peak, 1e-30)))


def encode_scale(power):
    return jnp.exp2(15.0 - power) * 0.999


def decode_scale(power):
    return jnp.exp2(power - 15.0) * (1.0 / 0.999)


def to_short(value):
    return jnp.floor(value + 0.5).astype(jnp.int32).astype(jnp.int16)


def from_short(value):
    return value.astype(jnp.int32).astype(F32)


def group_kernel(cells_ref, block_ref, mask_ref, out_ref, column_ref):
    sticks = mask_ref.shape[0]
    inside = jnp.where(mask_ref[...] > 0, 1.0, 0.0)
    lane = lax.broadcasted_iota(jnp.int32, (1, NG), 1)
    for s in range(sticks):
        cell = cells_ref[s]
        x, y = lax.shift_right_logical(cell, 7), jnp.bitwise_and(cell, NG - 1)
        column_ref[s : s + 1, :] = jnp.where(lane == 0, x, jnp.where(lane == 1, y, 0)).astype(F32)
    column = column_ref[...].astype(BF16)
    for group in range(GROUP):
        for line in range(2 * BANDS):
            value = block_ref[BANDS * group + line // 2, line % 2].astype(F32) * inside
            out_ref[group, line] = value.astype(BF16)
        out_ref[group, 2 * BANDS] = column


def spread_kernel(part_ref, high_ref, low_ref, rows_ref, out_ref, same_rows_ref):
    powers, tails = [], []
    for band in range(BANDS):
        real = part_ref[:, 2 * band].reshape(STICKS, NG)
        imag = part_ref[:, 2 * band + 1].reshape(STICKS, NG)
        both = jnp.concatenate([real, imag], axis=1)
        field = dot(high_ref[...], both, ((1,), (1,))) + dot(low_ref[...], both, ((1,), (1,)))
        power = exponent(jnp.max(jnp.abs(field), axis=0, keepdims=True))
        field = field * encode_scale(power)
        out_ref[:, 16 * band : 16 * band + 16, :] = to_short(field[:, :NG]).reshape(RING, 16, NG)
        rest = field[:, NG:].reshape(RING, 2, 8, STICKS - NG)
        tails += [rest[:, 0], rest[:, 1]]
        powers.append(power)
    cells = part_ref[:, 2 * BANDS].reshape(STICKS, NG)
    lane = lax.broadcasted_iota(jnp.int32, (8, NG), 1)
    pick = jnp.where(lane == 0, 128.0, jnp.where(lane == 1, 1.0, 0.0))
    flat = dot(pick.astype(BF16), cells, ((1,), (1,)))[0:1]
    index = lax.broadcasted_iota(jnp.int32, (8, NG), 0)
    notes = jnp.zeros((8, NG), F32)
    for place, line in enumerate((flat, *powers)):
        tail = jnp.concatenate([line[:, NG:], jnp.zeros((1, 2 * NG - STICKS), F32)], axis=1)
        notes = jnp.where(index == 2 * place, line[:, :NG], jnp.where(index == 2 * place + 1, tail, notes))
    notes = jnp.broadcast_to(notes[None], (RING, 8, NG))
    last = jnp.concatenate([jnp.concatenate(tails, axis=2), notes], axis=1)
    out_ref[:, 32:48, :] = to_short(last)


def plane_kernel(
    me_ref, recv_ref, v0_ref, v1_ref, v2_ref, v3_ref, stack_ref, wide_ref, xa_ref, xh_ref, fh_ref, fl_ref, order_ref, rows_ref,
    out_ref, same_rows_ref, val_ref, low_ref, cell_ref, onehot_ref, tall_ref, flat_ref, left_a_ref, left_b_ref, mid_ref, lift_ref, tail_ref, v_ref, v_sem,
):
    copies = [
        pltpu.make_async_copy(source, v_ref.at[turn], v_sem.at[turn])
        for turn, source in enumerate((v0_ref, v1_ref, v2_ref, v3_ref))
    ]
    for copy in copies:
        copy.start()

    for src in range(RING):
        val_ref[:, src * NG : (src + 1) * NG] = from_short(recv_ref[src, 0:32, :])
        last = from_short(recv_ref[src, 32:48, :])
        start = RING * NG + 32 * src
        for g in range(4):
            val_ref[8 * g : 8 * g + 8, start : start + 32] = last[:8, 32 * g : 32 * g + 32]
        for place in range(3):
            cell_ref[place : place + 1, src * NG : (src + 1) * NG] = last[8 + 2 * place : 9 + 2 * place]
            cell_ref[place : place + 1, start : start + 32] = last[9 + 2 * place : 10 + 2 * place, 0:32]

    cells = cell_ref[0:1, :].astype(jnp.int32)
    x_index = jnp.bitwise_and(lax.shift_right_logical(cells, 7) + RAD, NG - 1)
    y_index = jnp.bitwise_and(cells, NG - 1)
    onehot_ref[...] = jnp.where(
        lax.broadcasted_iota(jnp.int32, (WIN, ALL), 0) == x_index, 1.0, 0.0
    ).astype(BF16)
    pick_y = jnp.where(lax.broadcasted_iota(jnp.int32, (NG, ALL), 0) == y_index, 1.0, 0.0).astype(BF16)
    flat_ref[...] = dot(stack_ref[...], pick_y).astype(BF16)
    tall_ref[...] = dot(pick_y, wide_ref[...], ((0,), (0,))).astype(BF16)

    for band in range(BANDS):
        half = slice(16 * band, 16 * band + 16)
        value = val_ref[half, :] * decode_scale(cell_ref[1 + band : 2 + band, :])
        rounded = value.astype(BF16).astype(F32)
        low_ref[half, :] = value - rounded
        val_ref[half, :] = rounded

    lane = lax.broadcasted_iota(jnp.int32, (WIN, NG), 1)
    first = jnp.bitwise_and(lane, WIN - 1) == 0
    lower = lane < WIN

    def across(z, left_ref):
        for g in range(4):
            for part, ref in enumerate((val_ref, low_ref)):
                row = ref[pl.ds(8 * g + z, 1), :]
                spread = jnp.broadcast_to(row, (16, ALL)).astype(BF16)
                spread = jnp.concatenate([spread] * (WIN // 16), axis=0)
                at = (2 * g + part) * WIN
                left_ref[at : at + WIN, :] = spread * onehot_ref[...]
        full = dot(left_ref[...], tall_ref[...])
        full = full[:, :NG] + full[:, NG:]
        parts = [full[2 * g * WIN : (2 * g + 1) * WIN] + full[(2 * g + 1) * WIN : (2 * g + 2) * WIN] for g in range(4)]
        for band in range(BANDS):
            real, imag = parts[2 * band], parts[2 * band + 1]
            real_turn, imag_turn = pltpu.roll(real, WIN, 1), pltpu.roll(imag, WIN, 1)
            new_real = jnp.where(first, real, jnp.where(lower, real - imag_turn, real_turn + imag))
            new_imag = jnp.where(first, imag, jnp.where(lower, imag + real_turn, imag_turn - real))
            mid_ref[z, 0:WIN, band * NG : (band + 1) * NG] = new_real
            mid_ref[z, WIN:, band * NG : (band + 1) * NG] = new_imag

    @pl.loop(0, 4)
    def _(pair):
        across(2 * pair, left_a_ref)
        across(2 * pair + 1, left_b_ref)

    me = me_ref[0]
    for copy in copies:
        copy.wait()
    for turn in range(GROUP):
        for i in range(2):
            z = 2 * jnp.bitwise_xor(me, turn) + i
            at = i * NG
            potential = dot(v_ref[turn, at : at + NG, :], order_ref[...])
            potential += dot(v_ref[turn, at + 2 * NG : at + 3 * NG, :], order_ref[...])
            high, low = split(mid_ref[z])
            field = dot(xa_ref[...], jnp.concatenate([high, high], axis=0)) + dot(xh_ref[...], low)
            wide = jnp.concatenate([potential, potential], axis=1)
            weighted = field * jnp.concatenate([wide, wide], axis=0)
            high, low = split(weighted)
            folded = dot(fh_ref[...], high) + dot(fh_ref[...], low) + dot(fl_ref[...], high)
            for band in range(BANDS):
                real = folded[:WIN, band * NG : (band + 1) * NG]
                imag = folded[WIN:, band * NG : (band + 1) * NG]
                real_turn, imag_turn = pltpu.roll(real, WIN, 1), pltpu.roll(imag, WIN, 1)
                left_real = jnp.where(first, real, jnp.where(lower, real + real_turn, imag_turn - imag))
                left_imag = jnp.where(first, imag, jnp.where(lower, imag + imag_turn, real - real_turn))
                for part, value in enumerate((left_real, left_imag)):
                    high, low = split(value)
                    lift_ref[2 * band + part, z, :, 0:NG] = high
                    lift_ref[2 * band + part, z, :, NG:] = low

    @pl.loop(0, ALL // 256)
    def _(t):
        cols = pl.ds(pl.multiple_of(t * 256, 256), 256)
        select = onehot_ref[:, cols].astype(F32)[None]
        for g in range(4):
            rows = lift_ref[g].reshape(8 * WIN, 2 * NG)
            full = dot(rows, flat_ref[0:256, cols]) + dot(rows, flat_ref[256:512, cols])
            val_ref[8 * g : 8 * g + 8, cols] = jnp.sum(full.reshape(8, WIN, 256) * select, axis=1)

    for band in range(BANDS):
        half = slice(16 * band, 16 * band + 16)
        power = exponent(jnp.max(jnp.abs(val_ref[half, :]), axis=0, keepdims=True))
        cell_ref[1 + band : 2 + band, :] = power
        val_ref[half, :] = val_ref[half, :] * encode_scale(power)
    tail_ref[...] = jnp.zeros((RING, 16, NG), F32)
    for src in range(RING):
        out_ref[src, 0:32, :] = to_short(val_ref[:, src * NG : (src + 1) * NG])
        start = RING * NG + 32 * src
        for g in range(4):
            tail_ref[src, 0:8, 32 * g : 32 * g + 32] = val_ref[8 * g : 8 * g + 8, start : start + 32]
        for place in range(1, 3):
            tail_ref[src, 8 + 2 * place : 9 + 2 * place, :] = cell_ref[place : place + 1, src * NG : (src + 1) * NG]
            tail_ref[src, 9 + 2 * place : 10 + 2 * place, 0:32] = cell_ref[place : place + 1, start : start + 32]
    out_ref[:, 32:48, :] = to_short(tail_ref[...])


def finish_kernel(recv_ref, part_ref, high_ref, low_ref, out_ref, copies_ref, line_ref, pack_ref):
    squares = part_ref[:, 2 * BANDS].reshape(STICKS, NG).astype(F32)
    signed = jnp.where(squares < NG // 2, squares, squares - NG)
    across = signed * signed
    across = across[:, 0:1] + across[:, 1:2]
    k = lax.broadcasted_iota(jnp.int32, (STICKS, NG), 1)
    k = jnp.where(k < NG // 2, k, k - NG)
    total = across + (k * k).astype(F32)
    weight = jnp.where(total <= RAD * RAD, 1.0, 0.0)
    kinetic = 2.0 / (RAD * RAD) * total
    for band in range(BANDS):
        for src in range(RING):
            last = from_short(recv_ref[src, 32:48, :])
            main = from_short(recv_ref[src, 16 * band : 16 * band + 16, :])
            scale = decode_scale(last[10 + 2 * band : 12 + 2 * band])
            line_ref[16 * src : 16 * src + 16, 0:NG] = main * scale[0:1]
            for part in range(2):
                g = 2 * band + part
                at = 16 * src + 8 * part
                line_ref[at : at + 8, NG : NG + 32] = last[:8, 32 * g : 32 * g + 32] * scale[1:2, 0:32]
        high, low = split(jnp.transpose(line_ref[...])[:STICKS])
        product = dot(high, high_ref[...]) + dot(low, high_ref[...]) + dot(high, low_ref[...])
        for part in range(2):
            masked = part_ref[:, 2 * band + part].reshape(STICKS, NG).astype(F32)
            value = weight * (kinetic * masked + product[:, part * NG : (part + 1) * NG])
            value = value.reshape(GROUP, STICKS // GROUP, NG)
            out_ref[:, 2 * band + part] = value.astype(BF16)
            half = STICKS // GROUP // 2
            for src in range(GROUP):
                at = ((2 * band + part) * GROUP + src) * half
                turned = pltpu.roll(value[src, half:], NG // 2, 1)
                pack_ref[at : at + half, :] = value[src, :half] + turned
    packed = pack_ref[...].astype(BF16)
    for copy in range(copies_ref.shape[0]):
        copies_ref[copy] = packed


def vmem_call(kernel, out_shape, inputs, scratch=(), specs=None, outs=None, aliases=None):
    vmem = pl.BlockSpec(memory_space=pltpu.VMEM)
    return pl.pallas_call(
        kernel,
        out_shape=out_shape,
        in_specs=specs or [vmem] * len(inputs),
        out_specs=outs or jax.tree.map(lambda _: vmem, out_shape),
        input_output_aliases=aliases or {},
        scratch_shapes=list(scratch),
        compiler_params=pltpu.CompilerParams(vmem_limit_bytes=56 * 1024 * 1024),
    )(*inputs)


def group(stick_cells, block, sphere_mask):
    sticks = block.shape[2]
    shape = jax.ShapeDtypeStruct((GROUP, 2 * BANDS + 1, sticks, NG), BF16)
    whole = pl.BlockSpec(memory_space=pltpu.VMEM)
    specs = [pl.BlockSpec(memory_space=pltpu.SMEM), whole, whole]
    inputs = (stick_cells, block, sphere_mask)
    return vmem_call(group_kernel, shape, inputs, (pltpu.VMEM((sticks, NG), F32),), specs)


def spread(part, rows):
    (high, low), _ = depth_tables()
    shape = (
        jax.ShapeDtypeStruct((RING, ROWS, NG), jnp.int16),
        jax.ShapeDtypeStruct(rows.shape, rows.dtype),
    )
    whole, place = pl.BlockSpec(memory_space=pltpu.VMEM), pl.BlockSpec(memory_space=pl.ANY)
    inputs = (part, high, low, rows)
    return vmem_call(spread_kernel, shape, inputs, (), [whole] * 3 + [place], (whole, place), {3: 1})


def planes(me, recv, potentials, rows):
    stack, wide = across_tables()
    (xh, xl), (fh, fl) = down_tables()
    xa = np.concatenate([xh, xl], axis=1)
    shape = (jax.ShapeDtypeStruct((RING, ROWS, NG), jnp.int16), jax.ShapeDtypeStruct(rows.shape, rows.dtype))
    scratch = (
        pltpu.VMEM((32, ALL), F32),
        pltpu.VMEM((32, ALL), F32),
        pltpu.VMEM((8, ALL), F32),
        pltpu.VMEM((WIN, ALL), BF16),
        pltpu.VMEM((ALL, 2 * NG), BF16),
        pltpu.VMEM((4 * NG, ALL), BF16),
        pltpu.VMEM((8 * WIN, ALL), BF16),
        pltpu.VMEM((8 * WIN, ALL), BF16),
        pltpu.VMEM((8, 2 * WIN, 2 * NG), F32),
        pltpu.VMEM((4, 8, WIN, 2 * NG), BF16),
        pltpu.VMEM((RING, 16, NG), F32),
        pltpu.VMEM((GROUP, 4 * NG, NG), BF16),
        pltpu.SemaphoreType.DMA((GROUP,)),
    )
    inputs = (me, recv, *potentials, stack, wide, xa, xh, fh, fl, lane_order(), rows)
    whole = pl.BlockSpec(memory_space=pltpu.VMEM)
    specs = [pl.BlockSpec(memory_space=pltpu.SMEM), whole] + [pl.BlockSpec(memory_space=pl.ANY)] * GROUP
    specs += [whole] * (len(inputs) - 3 - GROUP) + [pl.BlockSpec(memory_space=pl.ANY)]
    outs = (whole, pl.BlockSpec(memory_space=pl.ANY))
    return vmem_call(plane_kernel, shape, inputs, scratch, specs, outs, {len(inputs) - 1: 1})


def finish(recv, part, copies):
    _, (high, low) = depth_tables()
    rows = BANDS * STICKS
    shape = (
        jax.ShapeDtypeStruct((GROUP, 2 * BANDS, STICKS // GROUP, NG), BF16),
        jax.ShapeDtypeStruct((copies, rows, NG), BF16),
    )
    scratch = (pltpu.VMEM((2 * NG, 2 * NG), F32), pltpu.VMEM((rows, NG), F32))
    return vmem_call(finish_kernel, shape, (recv, part, high, low), scratch)


def pack(value):
    half = value.shape[2] // 2
    return value[:, :, :half] + jnp.roll(value[:, :, half:], NG // 2, axis=3)


def pairing(bands, vectors, axis):
    full = 0.0
    for src, left in enumerate(bands):
        right = lax.index_in_dim(vectors, src, axis, False)
        full += jnp.einsum("rkl,gbqrl->kgbq", left, right, preferred_element_type=F32)
    full = full.reshape(-1, 2, *full.shape[1:])
    real = full[:, 0, :, :, 0] + full[:, 1, :, :, 1]
    imag = full[:, 0, :, :, 1] - full[:, 1, :, :, 0]
    return jnp.stack([real, imag])


def partner(value, turn, size):
    return lax.ppermute(value, "pw", [(i, i ^ turn) for i in range(size)])


def place(pieces, me):
    for bit in (1, 2):
        odd = jnp.bitwise_and(me, bit) != 0
        pieces = [jnp.where(odd, pieces[i ^ bit], pieces[i]) for i in range(GROUP)]
    return pieces


def exchange(value, axis, groups=None):
    return lax.all_to_all(value, axis, 0, 0, axis_index_groups=groups, tiled=True)


def to_all(value, axis, count, groups=None):
    return exchange(jnp.broadcast_to(value[None], (count, *value.shape)), axis, groups)


def per_device(block, bands, potential, stick_cells, sphere_mask):
    size = lax.axis_size("pw")
    teams = lax.axis_size("band")
    me = jnp.bitwise_and(lax.axis_index("pw"), GROUP - 1)
    own, sticks, rows = block.shape[0], block.shape[2], bands.shape[0]
    fours = [[i * GROUP + j for j in range(GROUP)] for i in range(size // GROUP)]
    rings = [[i * GROUP + j for i in range(size // GROUP)] for j in range(GROUP)]

    part = exchange(group(stick_cells, block, sphere_mask), "pw", fours)
    v_high = lax.reduce_precision(potential, 8, 7)
    v_low = (potential - v_high).astype(BF16)
    potential_rows = jnp.stack([v_high.astype(BF16), v_low]).reshape(-1, NG)
    sent, potential_rows = spread(part, potential_rows)
    recv = exchange(sent, "pw", rings)

    inside = sphere_mask.astype(BF16)[None, None]
    bands_rows = jnp.transpose(pack(bands * inside), (2, 0, 1, 3)).reshape(-1, NG)
    potentials = [potential_rows] + [partner(potential_rows, turn, size) for turn in range(1, GROUP)]
    back, bands_rows = planes(me.reshape(1), recv, potentials, bands_rows)
    back = exchange(back, "pw", rings)
    bands_all = place([bands_rows] + [partner(bands_rows, turn, size) for turn in range(1, GROUP)], me)
    bands_all = [piece.reshape(sticks // 2, 2 * rows, NG) for piece in bands_all]
    vectors = part[:, : 2 * BANDS].reshape(GROUP * BANDS, 2, sticks, NG)
    masked_all = lax.all_gather(jnp.stack([vectors, vectors]), "band", axis=1, tiled=True)[0]
    masked_all = pack(masked_all.reshape(teams * GROUP * BANDS, 2, sticks, NG))
    masked_all = masked_all.reshape(teams, GROUP, BANDS, 2, sticks // 2, NG)

    result, copies = finish(back, part, teams)
    applied_all = exchange(copies, "band").reshape(teams, BANDS, 2, GROUP, sticks // 2, NG)
    pieces = [lax.dynamic_index_in_dim(result, jnp.bitwise_xor(me, turn), 0, False) for turn in range(GROUP)]
    pieces = pieces[:1] + [partner(pieces[turn], turn, size) for turn in range(1, GROUP)]
    applied = jnp.stack(place(pieces, me)).reshape(own, 2, sticks, NG)

    terms = jnp.stack([pairing(bands_all, masked_all, 1), pairing(bands_all, applied_all, 3)])
    total = jnp.sum(to_all(terms.reshape(-1, NG), "pw", size // GROUP, rings), axis=0)
    total = to_all(total, "pw", GROUP, fours).reshape(GROUP, 2, 2, rows, teams, BANDS)
    total = jnp.transpose(total, (1, 2, 3, 4, 0, 5)).reshape(2, 2, rows, teams * own)
    return (applied, total[0], total[1])


def solution(mesh):
    return jax.shard_map(
        per_device,
        mesh=mesh,
        in_specs=(
            P("band", None, "pw", None),
            P("band", None, "pw", None),
            P("pw", None, None),
            P("pw"),
            P("pw", None),
        ),
        out_specs=(P("band", None, "pw", None), P(None, "band", None), P(None, "band", None)),
        check_vma=False,
    )
```

```python
import jax
import jax.numpy as jnp
import ml_dtypes
import numpy as np
from jax import lax
from jax.experimental import pallas as pl
from jax.experimental.pallas import tpu as pltpu
from jax.sharding import PartitionSpec as P

NG = 128
RAD = 32
WIN = 64
GROUP = 4
RING = 16
BANDS = 2
STICKS = 160
ROWS = 48
ALL = STICKS * RING
F32 = jnp.float32
BF16 = jnp.bfloat16


def split_table(table):
    high = table.astype(ml_dtypes.bfloat16)
    low = (table - high.astype(np.float64)).astype(ml_dtypes.bfloat16)
    return high, low


def angle(first, second):
    return 2.0 * np.pi / NG * np.mod(np.outer(first, second), NG)


def depth_tables():
    k = np.arange(NG)
    theta = angle(np.arange(NG), k)
    inverse = np.zeros((RING, 2, 8, 2 * NG))
    theta = theta.reshape(RING, 8, NG)
    inverse[:, 0] = np.concatenate([np.cos(theta), -np.sin(theta)], axis=-1)
    inverse[:, 1] = np.concatenate([np.sin(theta), np.cos(theta)], axis=-1)
    forward = np.zeros((RING, 2, 8, 2 * NG))
    forward[:, 0] = np.concatenate([np.cos(theta), -np.sin(theta)], axis=-1)
    forward[:, 1] = np.concatenate([np.sin(theta), np.cos(theta)], axis=-1)
    return split_table(inverse.reshape(2 * NG, 2 * NG)), split_table(forward.reshape(2 * NG, 2 * NG))


def across_tables():
    y = np.arange(NG)
    j = np.arange(WIN)
    theta = angle(j, y)
    lower = np.sin(theta)
    lower[0] = np.where(y % 2 == 0, 1.0, -1.0)
    high, low = split_table(np.concatenate([np.cos(theta), lower], axis=0))
    stacked = np.concatenate([high, high, low, low], axis=0)
    wide = np.concatenate([high.T, low.T], axis=1)
    return stacked, wide


def down_tables():
    freq = np.arange(WIN) - RAD
    theta = angle(np.arange(NG), freq)
    cosine, sine = np.cos(theta) / NG**3, np.sin(theta) / NG**3
    inverse = np.block([[cosine, -sine], [sine, cosine]])
    cosine, sine = np.cos(theta).T, np.sin(theta).T
    forward = np.block([[cosine, sine], [-sine, cosine]])
    return split_table(inverse), split_table(forward)


def lane_order():
    order = np.concatenate([np.arange(WIN), [WIN], np.arange(NG - 1, WIN, -1)])
    matrix = np.zeros((NG, NG))
    matrix[order, np.arange(NG)] = 1.0
    return matrix.astype(ml_dtypes.bfloat16)


def split(value):
    high = value.astype(BF16)
    low = (value - high.astype(F32)).astype(BF16)
    return high, low


def dot(left, right, dims=((1,), (0,))):
    return lax.dot_general(left, right, (dims, ((), ())), preferred_element_type=F32)


def exponent(peak):
    return jnp.ceil(jnp.log2(jnp.maximum(peak, 1e-30)))


def encode_scale(power):
    return jnp.exp2(15.0 - power) * 0.999


def decode_scale(power):
    return jnp.exp2(power - 15.0) * (1.0 / 0.999)


def to_short(value):
    return jnp.floor(value + 0.5).astype(jnp.int32).astype(jnp.int16)


def from_short(value):
    return value.astype(jnp.int32).astype(F32)


def group_kernel(cells_ref, block_ref, mask_ref, out_ref, column_ref):
    sticks = mask_ref.shape[0]
    inside = jnp.where(mask_ref[...] > 0, 1.0, 0.0)
    lane = lax.broadcasted_iota(jnp.int32, (1, NG), 1)
    for s in range(sticks):
        cell = cells_ref[s]
        x, y = lax.shift_right_logical(cell, 7), jnp.bitwise_and(cell, NG - 1)
        column_ref[s : s + 1, :] = jnp.where(lane == 0, x, jnp.where(lane == 1, y, 0)).astype(F32)
    column = column_ref[...].astype(BF16)
    for group in range(GROUP):
        for line in range(2 * BANDS):
            value = block_ref[BANDS * group + line // 2, line % 2].astype(F32) * inside
            out_ref[group, line] = value.astype(BF16)
        out_ref[group, 2 * BANDS] = column


def spread_kernel(part_ref, high_ref, low_ref, rows_ref, out_ref, same_rows_ref):
    powers, tails = [], []
    for band in range(BANDS):
        real = part_ref[:, 2 * band].reshape(STICKS, NG)
        imag = part_ref[:, 2 * band + 1].reshape(STICKS, NG)
        both = jnp.concatenate([real, imag], axis=1)
        field = dot(high_ref[...], both, ((1,), (1,))) + dot(low_ref[...], both, ((1,), (1,)))
        power = exponent(jnp.max(jnp.abs(field), axis=0, keepdims=True))
        field = field * encode_scale(power)
        out_ref[:, 16 * band : 16 * band + 16, :] = to_short(field[:, :NG]).reshape(RING, 16, NG)
        rest = field[:, NG:].reshape(RING, 2, 8, STICKS - NG)
        tails += [rest[:, 0], rest[:, 1]]
        powers.append(power)
    cells = part_ref[:, 2 * BANDS].reshape(STICKS, NG)
    lane = lax.broadcasted_iota(jnp.int32, (8, NG), 1)
    pick = jnp.where(lane == 0, 128.0, jnp.where(lane == 1, 1.0, 0.0))
    flat = dot(pick.astype(BF16), cells, ((1,), (1,)))[0:1]
    index = lax.broadcasted_iota(jnp.int32, (8, NG), 0)
    notes = jnp.zeros((8, NG), F32)
    for place, line in enumerate((flat, *powers)):
        tail = jnp.concatenate([line[:, NG:], jnp.zeros((1, 2 * NG - STICKS), F32)], axis=1)
        notes = jnp.where(index == 2 * place, line[:, :NG], jnp.where(index == 2 * place + 1, tail, notes))
    notes = jnp.broadcast_to(notes[None], (RING, 8, NG))
    last = jnp.concatenate([jnp.concatenate(tails, axis=2), notes], axis=1)
    out_ref[:, 32:48, :] = to_short(last)


def plane_kernel(
    me_ref, recv_ref, v0_ref, v1_ref, v2_ref, v3_ref, stack_ref, wide_ref, xa_ref, xh_ref, fh_ref, fl_ref, order_ref, rows_ref,
    out_ref, same_rows_ref, val_ref, low_ref, cell_ref, onehot_ref, tall_ref, flat_ref, left_a_ref, left_b_ref, mid_ref, lift_ref, tail_ref, v_ref, v_sem,
):
    copies = [
        pltpu.make_async_copy(source, v_ref.at[turn], v_sem.at[turn])
        for turn, source in enumerate((v0_ref, v1_ref, v2_ref, v3_ref))
    ]
    for copy in copies:
        copy.start()

    for src in range(RING):
        val_ref[:, src * NG : (src + 1) * NG] = from_short(recv_ref[src, 0:32, :])
        last = from_short(recv_ref[src, 32:48, :])
        start = RING * NG + 32 * src
        for g in range(4):
            val_ref[8 * g : 8 * g + 8, start : start + 32] = last[:8, 32 * g : 32 * g + 32]
        for place in range(3):
            cell_ref[place : place + 1, src * NG : (src + 1) * NG] = last[8 + 2 * place : 9 + 2 * place]
            cell_ref[place : place + 1, start : start + 32] = last[9 + 2 * place : 10 + 2 * place, 0:32]

    cells = cell_ref[0:1, :].astype(jnp.int32)
    x_index = jnp.bitwise_and(lax.shift_right_logical(cells, 7) + RAD, NG - 1)
    y_index = jnp.bitwise_and(cells, NG - 1)
    onehot_ref[...] = jnp.where(
        lax.broadcasted_iota(jnp.int32, (WIN, ALL), 0) == x_index, 1.0, 0.0
    ).astype(BF16)
    pick_y = jnp.where(lax.broadcasted_iota(jnp.int32, (NG, ALL), 0) == y_index, 1.0, 0.0).astype(BF16)
    flat_ref[...] = dot(stack_ref[...], pick_y).astype(BF16)
    tall_ref[...] = dot(pick_y, wide_ref[...], ((0,), (0,))).astype(BF16)

    for band in range(BANDS):
        half = slice(16 * band, 16 * band + 16)
        value = val_ref[half, :] * decode_scale(cell_ref[1 + band : 2 + band, :])
        rounded = value.astype(BF16).astype(F32)
        low_ref[half, :] = value - rounded
        val_ref[half, :] = rounded

    lane = lax.broadcasted_iota(jnp.int32, (WIN, NG), 1)
    first = jnp.bitwise_and(lane, WIN - 1) == 0
    lower = lane < WIN

    def across(z, left_ref):
        for g in range(4):
            for part, ref in enumerate((val_ref, low_ref)):
                row = ref[pl.ds(8 * g + z, 1), :]
                spread = jnp.broadcast_to(row, (16, ALL)).astype(BF16)
                spread = jnp.concatenate([spread] * (WIN // 16), axis=0)
                at = (2 * g + part) * WIN
                left_ref[at : at + WIN, :] = spread * onehot_ref[...]
        full = dot(left_ref[...], tall_ref[...])
        full = full[:, :NG] + full[:, NG:]
        parts = [full[2 * g * WIN : (2 * g + 1) * WIN] + full[(2 * g + 1) * WIN : (2 * g + 2) * WIN] for g in range(4)]
        for band in range(BANDS):
            real, imag = parts[2 * band], parts[2 * band + 1]
            real_turn, imag_turn = pltpu.roll(real, WIN, 1), pltpu.roll(imag, WIN, 1)
            new_real = jnp.where(first, real, jnp.where(lower, real - imag_turn, real_turn + imag))
            new_imag = jnp.where(first, imag, jnp.where(lower, imag + real_turn, imag_turn - real))
            mid_ref[z, 0:WIN, band * NG : (band + 1) * NG] = new_real
            mid_ref[z, WIN:, band * NG : (band + 1) * NG] = new_imag

    @pl.loop(0, 4)
    def _(pair):
        across(2 * pair, left_a_ref)
        across(2 * pair + 1, left_b_ref)

    me = me_ref[0]
    for copy in copies:
        copy.wait()
    for owner in range(GROUP):
        turn = jnp.bitwise_xor(me, owner)
        for i in range(2):
            z = 2 * owner + i
            at = i * NG
            potential = dot(v_ref[turn, at : at + NG, :], order_ref[...])
            potential += dot(v_ref[turn, at + 2 * NG : at + 3 * NG, :], order_ref[...])
            high, low = split(mid_ref[z])
            field = dot(xa_ref[...], jnp.concatenate([high, high], axis=0)) + dot(xh_ref[...], low)
            wide = jnp.concatenate([potential, potential], axis=1)
            weighted = field * jnp.concatenate([wide, wide], axis=0)
            high, low = split(weighted)
            folded = dot(fh_ref[...], high) + dot(fh_ref[...], low) + dot(fl_ref[...], high)
            for band in range(BANDS):
                real = folded[:WIN, band * NG : (band + 1) * NG]
                imag = folded[WIN:, band * NG : (band + 1) * NG]
                real_turn, imag_turn = pltpu.roll(real, WIN, 1), pltpu.roll(imag, WIN, 1)
                left_real = jnp.where(first, real, jnp.where(lower, real + real_turn, imag_turn - imag))
                left_imag = jnp.where(first, imag, jnp.where(lower, imag + imag_turn, real - real_turn))
                for part, value in enumerate((left_real, left_imag)):
                    high, low = split(value)
                    lift_ref[2 * band + part, z, :, 0:NG] = high
                    lift_ref[2 * band + part, z, :, NG:] = low

    @pl.loop(0, ALL // 256)
    def _(t):
        cols = pl.ds(pl.multiple_of(t * 256, 256), 256)
        select = onehot_ref[:, cols].astype(F32)[None]
        for g in range(4):
            rows = lift_ref[g].reshape(8 * WIN, 2 * NG)
            full = dot(rows, flat_ref[0:256, cols]) + dot(rows, flat_ref[256:512, cols])
            val_ref[8 * g : 8 * g + 8, cols] = jnp.sum(full.reshape(8, WIN, 256) * select, axis=1)

    for band in range(BANDS):
        half = slice(16 * band, 16 * band + 16)
        power = exponent(jnp.max(jnp.abs(val_ref[half, :]), axis=0, keepdims=True))
        cell_ref[1 + band : 2 + band, :] = power
        val_ref[half, :] = val_ref[half, :] * encode_scale(power)
    tail_ref[...] = jnp.zeros((RING, 16, NG), F32)
    for src in range(RING):
        out_ref[src, 0:32, :] = to_short(val_ref[:, src * NG : (src + 1) * NG])
        start = RING * NG + 32 * src
        for g in range(4):
            tail_ref[src, 0:8, 32 * g : 32 * g + 32] = val_ref[8 * g : 8 * g + 8, start : start + 32]
        for place in range(1, 3):
            tail_ref[src, 8 + 2 * place : 9 + 2 * place, :] = cell_ref[place : place + 1, src * NG : (src + 1) * NG]
            tail_ref[src, 9 + 2 * place : 10 + 2 * place, 0:32] = cell_ref[place : place + 1, start : start + 32]
    out_ref[:, 32:48, :] = to_short(tail_ref[...])


def finish_kernel(recv_ref, part_ref, high_ref, low_ref, out_ref, copies_ref, line_ref, pack_ref):
    squares = part_ref[:, 2 * BANDS].reshape(STICKS, NG).astype(F32)
    signed = jnp.where(squares < NG // 2, squares, squares - NG)
    across = signed * signed
    across = across[:, 0:1] + across[:, 1:2]
    k = lax.broadcasted_iota(jnp.int32, (STICKS, NG), 1)
    k = jnp.where(k < NG // 2, k, k - NG)
    total = across + (k * k).astype(F32)
    weight = jnp.where(total <= RAD * RAD, 1.0, 0.0)
    kinetic = 2.0 / (RAD * RAD) * total
    for band in range(BANDS):
        for src in range(RING):
            last = from_short(recv_ref[src, 32:48, :])
            main = from_short(recv_ref[src, 16 * band : 16 * band + 16, :])
            scale = decode_scale(last[10 + 2 * band : 12 + 2 * band])
            line_ref[16 * src : 16 * src + 16, 0:NG] = main * scale[0:1]
            for part in range(2):
                g = 2 * band + part
                at = 16 * src + 8 * part
                line_ref[at : at + 8, NG : NG + 32] = last[:8, 32 * g : 32 * g + 32] * scale[1:2, 0:32]
        high, low = split(jnp.transpose(line_ref[...])[:STICKS])
        product = dot(high, high_ref[...]) + dot(low, high_ref[...]) + dot(high, low_ref[...])
        for part in range(2):
            masked = part_ref[:, 2 * band + part].reshape(STICKS, NG).astype(F32)
            value = weight * (kinetic * masked + product[:, part * NG : (part + 1) * NG])
            value = value.reshape(GROUP, STICKS // GROUP, NG)
            out_ref[:, 2 * band + part] = value.astype(BF16)
            half = STICKS // GROUP // 2
            for src in range(GROUP):
                at = ((2 * band + part) * GROUP + src) * half
                turned = pltpu.roll(value[src, half:], NG // 2, 1)
                pack_ref[at : at + half, :] = value[src, :half] + turned
    packed = pack_ref[...].astype(BF16)
    for copy in range(copies_ref.shape[0]):
        copies_ref[copy] = packed


def vmem_call(kernel, out_shape, inputs, scratch=(), specs=None, outs=None, aliases=None):
    vmem = pl.BlockSpec(memory_space=pltpu.VMEM)
    return pl.pallas_call(
        kernel,
        out_shape=out_shape,
        in_specs=specs or [vmem] * len(inputs),
        out_specs=outs or jax.tree.map(lambda _: vmem, out_shape),
        input_output_aliases=aliases or {},
        scratch_shapes=list(scratch),
        compiler_params=pltpu.CompilerParams(vmem_limit_bytes=56 * 1024 * 1024),
    )(*inputs)


def group(stick_cells, block, sphere_mask):
    sticks = block.shape[2]
    shape = jax.ShapeDtypeStruct((GROUP, 2 * BANDS + 1, sticks, NG), BF16)
    whole = pl.BlockSpec(memory_space=pltpu.VMEM)
    specs = [pl.BlockSpec(memory_space=pltpu.SMEM), whole, whole]
    inputs = (stick_cells, block, sphere_mask)
    return vmem_call(group_kernel, shape, inputs, (pltpu.VMEM((sticks, NG), F32),), specs)


def spread(part, rows):
    (high, low), _ = depth_tables()
    shape = (
        jax.ShapeDtypeStruct((RING, ROWS, NG), jnp.int16),
        jax.ShapeDtypeStruct(rows.shape, rows.dtype),
    )
    whole, place = pl.BlockSpec(memory_space=pltpu.VMEM), pl.BlockSpec(memory_space=pl.ANY)
    inputs = (part, high, low, rows)
    return vmem_call(spread_kernel, shape, inputs, (), [whole] * 3 + [place], (whole, place), {3: 1})


def planes(me, recv, potentials, rows):
    stack, wide = across_tables()
    (xh, xl), (fh, fl) = down_tables()
    xa = np.concatenate([xh, xl], axis=1)
    shape = (jax.ShapeDtypeStruct((RING, ROWS, NG), jnp.int16), jax.ShapeDtypeStruct(rows.shape, rows.dtype))
    scratch = (
        pltpu.VMEM((32, ALL), F32),
        pltpu.VMEM((32, ALL), F32),
        pltpu.VMEM((8, ALL), F32),
        pltpu.VMEM((WIN, ALL), BF16),
        pltpu.VMEM((ALL, 2 * NG), BF16),
        pltpu.VMEM((4 * NG, ALL), BF16),
        pltpu.VMEM((8 * WIN, ALL), BF16),
        pltpu.VMEM((8 * WIN, ALL), BF16),
        pltpu.VMEM((8, 2 * WIN, 2 * NG), F32),
        pltpu.VMEM((4, 8, WIN, 2 * NG), BF16),
        pltpu.VMEM((RING, 16, NG), F32),
        pltpu.VMEM((GROUP, 4 * NG, NG), BF16),
        pltpu.SemaphoreType.DMA((GROUP,)),
    )
    inputs = (me, recv, *potentials, stack, wide, xa, xh, fh, fl, lane_order(), rows)
    whole = pl.BlockSpec(memory_space=pltpu.VMEM)
    specs = [pl.BlockSpec(memory_space=pltpu.SMEM), whole] + [pl.BlockSpec(memory_space=pl.ANY)] * GROUP
    specs += [whole] * (len(inputs) - 3 - GROUP) + [pl.BlockSpec(memory_space=pl.ANY)]
    outs = (whole, pl.BlockSpec(memory_space=pl.ANY))
    return vmem_call(plane_kernel, shape, inputs, scratch, specs, outs, {len(inputs) - 1: 1})


def finish(recv, part, copies):
    _, (high, low) = depth_tables()
    rows = BANDS * STICKS
    shape = (
        jax.ShapeDtypeStruct((GROUP, 2 * BANDS, STICKS // GROUP, NG), BF16),
        jax.ShapeDtypeStruct((copies, rows, NG), BF16),
    )
    scratch = (pltpu.VMEM((2 * NG, 2 * NG), F32), pltpu.VMEM((rows, NG), F32))
    return vmem_call(finish_kernel, shape, (recv, part, high, low), scratch)


def pack(value):
    half = value.shape[2] // 2
    return value[:, :, :half] + jnp.roll(value[:, :, half:], NG // 2, axis=3)


def pairing(bands, vectors, axis):
    full = 0.0
    for src, left in enumerate(bands):
        right = lax.index_in_dim(vectors, src, axis, False)
        full += jnp.einsum("rkl,gbqrl->kgbq", left, right, preferred_element_type=F32)
    full = full.reshape(-1, 2, *full.shape[1:])
    real = full[:, 0, :, :, 0] + full[:, 1, :, :, 1]
    imag = full[:, 0, :, :, 1] - full[:, 1, :, :, 0]
    return jnp.stack([real, imag])


def partner(value, turn, size):
    return lax.ppermute(value, "pw", [(i, i ^ turn) for i in range(size)])


def place(pieces, me):
    for bit in (1, 2):
        odd = jnp.bitwise_and(me, bit) != 0
        pieces = [jnp.where(odd, pieces[i ^ bit], pieces[i]) for i in range(GROUP)]
    return pieces


def exchange(value, axis, groups=None):
    return lax.all_to_all(value, axis, 0, 0, axis_index_groups=groups, tiled=True)


def to_all(value, axis, count, groups=None):
    return exchange(jnp.broadcast_to(value[None], (count, *value.shape)), axis, groups)


def per_device(block, bands, potential, stick_cells, sphere_mask):
    size = lax.axis_size("pw")
    teams = lax.axis_size("band")
    me = jnp.bitwise_and(lax.axis_index("pw"), GROUP - 1)
    own, sticks, rows = block.shape[0], block.shape[2], bands.shape[0]
    fours = [[i * GROUP + j for j in range(GROUP)] for i in range(size // GROUP)]
    rings = [[i * GROUP + j for i in range(size // GROUP)] for j in range(GROUP)]

    part = exchange(group(stick_cells, block, sphere_mask), "pw", fours)
    v_high = lax.reduce_precision(potential, 8, 7)
    v_low = (potential - v_high).astype(BF16)
    potential_rows = jnp.stack([v_high.astype(BF16), v_low]).reshape(-1, NG)
    sent, potential_rows = spread(part, potential_rows)
    recv = exchange(sent, "pw", rings)

    inside = sphere_mask.astype(BF16)[None, None]
    bands_rows = jnp.transpose(pack(bands * inside), (2, 0, 1, 3)).reshape(-1, NG)
    potentials = [potential_rows] + [partner(potential_rows, turn, size) for turn in range(1, GROUP)]
    back, bands_rows = planes(me.reshape(1), recv, potentials, bands_rows)
    back = exchange(back, "pw", rings)
    bands_all = place([bands_rows] + [partner(bands_rows, turn, size) for turn in range(1, GROUP)], me)
    bands_all = [piece.reshape(sticks // 2, 2 * rows, NG) for piece in bands_all]
    vectors = part[:, : 2 * BANDS].reshape(GROUP * BANDS, 2, sticks, NG)
    masked_all = lax.all_gather(jnp.stack([vectors, vectors]), "band", axis=1, tiled=True)[0]
    masked_all = pack(masked_all.reshape(teams * GROUP * BANDS, 2, sticks, NG))
    masked_all = masked_all.reshape(teams, GROUP, BANDS, 2, sticks // 2, NG)

    result, copies = finish(back, part, teams)
    applied_all = exchange(copies, "band").reshape(teams, BANDS, 2, GROUP, sticks // 2, NG)
    pieces = [lax.dynamic_index_in_dim(result, jnp.bitwise_xor(me, turn), 0, False) for turn in range(GROUP)]
    pieces = pieces[:1] + [partner(pieces[turn], turn, size) for turn in range(1, GROUP)]
    applied = jnp.stack(place(pieces, me)).reshape(own, 2, sticks, NG)

    terms = jnp.stack([pairing(bands_all, masked_all, 1), pairing(bands_all, applied_all, 3)])
    total = jnp.sum(to_all(terms.reshape(-1, NG), "pw", size // GROUP, rings), axis=0)
    total = to_all(total, "pw", GROUP, fours).reshape(GROUP, 2, 2, rows, teams, BANDS)
    total = jnp.transpose(total, (1, 2, 3, 4, 0, 5)).reshape(2, 2, rows, teams * own)
    return (applied, total[0], total[1])


def solution(mesh):
    return jax.shard_map(
        per_device,
        mesh=mesh,
        in_specs=(
            P("band", None, "pw", None),
            P("band", None, "pw", None),
            P("pw", None, None),
            P("pw"),
            P("pw", None),
        ),
        out_specs=(P("band", None, "pw", None), P(None, "band", None), P(None, "band", None)),
        check_vma=False,
    )
```
